256 devices in a mesh: leaf: 64 (over z, x, core), rhs: 4 (over y).
Axes of the slice: x: 4, y: 4, z: 8, core: 2. Of those that a mesh axis runs over, the one named last changes fastest.
Arguments:
- rhs_block: bfloat16 [256, 131072], P('rhs', 'leaf'), may hold values from -6 to 6
- leaf_basis: bfloat16 [131072, 128], P('leaf'), may hold values from -0.5 to 0.5
- local_transfer: bfloat16 [64, 30, 128, 128], P('leaf'), may hold values from -0.375 to 0.375
- top_transfer: bfloat16 [120, 128, 128], replicated, may hold values from -0.375 to 0.375
- coupling_tiles: bfloat16 [64, 128, 128], P('rhs'), may hold values from -0.1875 to 0.1875
- send_index: int32 [64, 64, 4], replicated, may hold values from -1 to 15, as said below
- leaf_list: int32 [2, 1024, 192], P(None, 'leaf'), may hold values from 0 to 255, as said below
- top_list: int32 [3, 512], replicated, may hold values from 0 to 127, as said below
Outputs:
- far_field: bfloat16 [256, 131072], P('rhs', 'leaf')
The draws below stay inside these ranges and needn't reach their ends.
Inputs may be any that keep to these rules, and one draw needn't show every extreme that they name: `send_index`: each slot holds a distinct local leaf of the sender or -1; the used slots of a pair come first and the rest are -1; every device fills all 4 slots to itself. `leaf_list`: every slot named in [0] holds a leaf (not -1) for the receiving device that owns the target leaf. `top_list`: target and source lie on the same level of the top tree, at least level 2, and differ by two or more places cyclically within it.
All inputs are finite; a program needn't handle non-finite values.
Results may differ from the reference program's by a relative error of at most 0.017.
Values may be sent and summed in bfloat16 or wider, within the bound.
No kernel may reach another device: no remote copies, remote signals or barrier semaphores. Data moves between devices by JAX's collectives and lax.ppermute only.
A program may use at most 192 MiB of HBM per device.

```python
import jax
import jax.numpy as jnp
from jax import lax

RANK = 128
R = 256
M = 128
LOG_LD = 4
C = 4
ENT = 192
TILES = 64
LD = 16
LEAVES = 1024
NPTS = 131072
TOPE = 512
N_LEAF = 64


def common_lists(key):
    base = jax.random.fold_in(key, 7301)
    key_count = jax.random.fold_in(base, 1)
    key_perm = jax.random.fold_in(base, 2)
    key_pick = jax.random.fold_in(base, 3)
    key_tile = jax.random.fold_in(base, 4)
    counts = jax.random.randint(key_count, (N_LEAF, N_LEAF), 0, C + 1)
    diag = jnp.arange(N_LEAF)[:, None] == jnp.arange(N_LEAF)[None, :]
    counts = jnp.where(diag, C, counts).astype(jnp.int32)
    keys = jax.random.split(key_perm, N_LEAF * N_LEAF)
    perms = jax.vmap(lambda k: jax.random.permutation(k, LD))(keys).reshape(N_LEAF, N_LEAF, LD)[:, :, :C]
    used = jnp.arange(C)[None, None, :] < counts[:, :, None]
    sends = jnp.where(used, perms, -1).astype(jnp.int32)
    live = jnp.transpose(used, (1, 0, 2)).reshape(N_LEAF, N_LEAF * C).astype(jnp.int32)
    total = jnp.sum(live, axis=1)
    picks = jax.random.randint(key_pick, (N_LEAF, LD * ENT), 0, total[:, None])
    running = jnp.cumsum(live, axis=1)
    slots = jax.vmap(lambda row, want: jnp.searchsorted(row, want + 1, side='left'))(running, picks)
    slots = slots.reshape(LEAVES, ENT).astype(jnp.int32)
    tiles = jax.random.randint(key_tile, (LEAVES, ENT), 0, TILES).astype(jnp.int32)
    return (sends, jnp.stack([slots, tiles]))


def draw_send_index(key, part):
    return common_lists(key)[0]


def draw_leaf_list(key, part):
    return common_lists(key)[1]


def draw_top_list(key, part):
    base = jax.random.fold_in(key, 9113)
    target = jax.random.randint(jax.random.fold_in(base, 1), (TOPE,), 4, 2 * N_LEAF)
    start = jnp.full((TOPE,), 4, jnp.int32)
    power = 8
    while power <= N_LEAF:
        start = jnp.where(target >= power, power, start)
        power = power * 2
    extra = jax.random.randint(jax.random.fold_in(base, 2), (TOPE,), 0, start - 3)
    source = start + (target - start + 2 + extra) % start
    tile = jax.random.randint(jax.random.fold_in(base, 3), (TOPE,), 0, TILES)
    return jnp.stack([target, source, tile]).astype(jnp.int32)


def block_scale(stream_key, extent, shards, smallest, largest):
    loudness = 1.0
    for dim, shards_of in shards:
        steps = jax.random.uniform(jax.random.fold_in(jax.random.fold_in(stream_key, 6), dim), (shards_of,), jnp.float32, smallest / len(shards), largest / len(shards))
        loudness = loudness * jnp.repeat(jnp.exp(steps), extent[dim] // shards_of).reshape((-1,) + (1,) * (len(extent) - 1 - dim))
    return loudness


def scatter_about(stream_key, shape, spread, bound, shards=(), held_as=jnp.bfloat16):
    drawn = jax.random.normal(stream_key, shape, jnp.float32) * spread
    if len(shards) > 0:
        drawn = block_scale(stream_key, shape, shards, -0.22, 0.18) * drawn
    return jnp.clip(drawn, min=-bound, max=bound).astype(held_as)


def setup_inputs(seed: int = 0) -> dict:
    key_of = jax.random.split(jax.random.key(seed), 9)
    rhs_block = scatter_about(key_of[0], (R, NPTS), 1.0, 6.0, ((0, 4), (1, 64)))
    leaf_basis = scatter_about(key_of[1], (NPTS, RANK), M ** -0.5, 0.5, ((0, 64),))
    local_transfer = scatter_about(key_of[2], (N_LEAF, 2 * LD - 2, RANK, RANK), (2 * RANK) ** -0.5, 0.375, ((0, 64),))
    top_transfer = scatter_about(key_of[3], (2 * N_LEAF - 8, RANK, RANK), (2 * RANK) ** -0.5, 0.375)
    coupling_tiles = scatter_about(key_of[4], (TILES, RANK, RANK), (8 * RANK) ** -0.5, 0.1875, ((0, 4),))
    send_index = draw_send_index(jax.random.fold_in(key_of[8], 71), 0)
    leaf_list = draw_leaf_list(jax.random.fold_in(key_of[8], 71), 0)
    top_list = draw_top_list(jax.random.fold_in(key_of[8], 71), 0)
    return dict(rhs_block=rhs_block, leaf_basis=leaf_basis, local_transfer=local_transfer, top_transfer=top_transfer, coupling_tiles=coupling_tiles, send_index=send_index, leaf_list=leaf_list, top_list=top_list)


def reference(rhs_block, leaf_basis, local_transfer, top_transfer, coupling_tiles, send_index, leaf_list, top_list):
    f32 = jnp.float32
    bf16 = jnp.bfloat16
    ltop = N_LEAF.bit_length() - 1
    points = rhs_block.reshape(R, LEAVES, M).astype(f32)
    basis = leaf_basis.reshape(LEAVES, M, RANK).astype(f32)
    xleaf = jnp.einsum("blm,lmq->lbq", points, basis).astype(bf16)
    panels = xleaf.reshape(N_LEAF, LD, R, RANK)
    count = LD
    while count > 1:
        trans = local_transfer[:, count - 2:2 * count - 2].astype(f32)
        prods = jnp.einsum("nhbr,nhrq->nhbq", panels.astype(f32), trans)
        panels = prods.reshape(N_LEAF, count // 2, 2, R, RANK).sum(axis=2).astype(bf16)
        count = count // 2
    xtop = jnp.zeros((2 * N_LEAF, R, RANK), bf16)
    xtop = xtop.at[N_LEAF:].set(panels[:, 0])
    for level in range(ltop - 1, 1, -1):
        lo = 2 ** (level + 1)
        child = xtop[lo:2 * lo].astype(f32)
        trans = top_transfer[lo - 8:2 * lo - 8].astype(f32)
        prods = jnp.einsum("cbr,crq->cbq", child, trans)
        parent = prods.reshape(lo // 2, 2, R, RANK).sum(axis=1).astype(bf16)
        xtop = xtop.at[lo // 2:lo].set(parent)
    tgt = top_list[0]
    src = top_list[1]
    til = top_list[2]
    contrib = jnp.einsum("ebr,erq->ebq", xtop[src].astype(f32), coupling_tiles[til].astype(f32))
    ytop = jnp.zeros((2 * N_LEAF, R, RANK), f32).at[tgt].add(contrib)
    for level in range(3, ltop + 1):
        lo = 2 ** level
        parent = jnp.repeat(ytop[lo // 2:lo].astype(bf16), 2, axis=0).astype(f32)
        trans = top_transfer[lo - 8:2 * lo - 8].astype(f32)
        ytop = ytop.at[lo:2 * lo].add(jnp.einsum("cbq,crq->cbr", parent, trans))
    ydown = ytop[N_LEAF:][:, None]
    for level in range(1, LOG_LD + 1):
        lo = 2 ** level
        parent = jnp.repeat(ydown.astype(bf16), 2, axis=1).astype(f32)
        trans = local_transfer[:, lo - 2:2 * lo - 2].astype(f32)
        ydown = jnp.einsum("nhbq,nhrq->nhbr", parent, trans)
    ydown = ydown.reshape(LEAVES, R, RANK)
    slots = leaf_list[0]
    owner = (jnp.arange(LEAVES, dtype=jnp.int32) // LD)[:, None]
    sender = slots // C
    place = slots % C
    source = sender * LD + send_index[sender, owner, place]

    def couple(args):
        index, tile = args
        return jnp.einsum("ebr,erq->bq", xleaf[index].astype(f32), coupling_tiles[tile].astype(f32))

    coupled = lax.map(couple, (source, leaf_list[1]))
    wleaf = (ydown + coupled).astype(bf16)
    out = jnp.einsum("lbq,lmq->blm", wleaf.astype(f32), basis)
    return out.reshape(R, NPTS).astype(bf16)
```

```python
import functools

import jax
import jax.numpy as jnp
from jax import lax
from jax.experimental import pallas as pl
from jax.experimental.pallas import tpu as pltpu
from jax.sharding import Mesh, PartitionSpec as P

F32 = jnp.float32
BF16 = jnp.bfloat16
RANK = 128
LD = 16
TILES = 64
GROUP = 16
ROWS = 4
TARGETS = 48
LANES = ROWS * RANK
VMEM_LIMIT = 60 * 1024 * 1024


def mm(a, b):
    return jnp.dot(a, b, preferred_element_type=F32)


def mm_nt(a, b):
    return lax.dot_general(a, b, (((1,), (1,)), ((), ())), preferred_element_type=F32)


def gather_kernel(xme, rhs, basis, trans, lists, msg, panels, root):
    x = xme[0]
    current = []
    for g in range(LD):
        panel = mm(rhs[:, g * RANK : (g + 1) * RANK], basis[g * RANK : (g + 1) * RANK, :])
        panels[g * 64 : (g + 1) * 64, :] = panel
        current.append(panel.astype(BF16))
    count = LD
    while count > 1:
        above = []
        for h in range(count // 2):
            pair = jnp.concatenate([current[2 * h], current[2 * h + 1]], axis=1)
            at = count - 2 + 2 * h
            above.append(mm(pair, trans[at : at + 2].reshape(2 * RANK, RANK)))
        current = [a.astype(BF16) for a in above]
        count //= 2
    root[...] = jnp.zeros_like(root)
    root[0:64, :] = above[0]
    slot = lists[0]
    p = slot >> 2
    slot = ((x - (p >> 1)) & 3) * 64 + (p >> 3) * 8 + (p & 1) * 4 + (slot & 3)
    slot = slot.astype(F32).astype(BF16)
    tile = lists[1].astype(F32).astype(BF16)
    none = jnp.full((LD, RANK), -1.0, BF16)
    for j in range(GROUP):
        msg[j, :, 128:256] = none
        msg[j, :, 0:192] = slot
        msg[j, :, 384:512] = none
        msg[j, :, 256:448] = tile
        for r in range(ROWS):
            msg[j, :, 512 + r * RANK : 512 + (r + 1) * RANK] = panels[
                pl.ds(r * GROUP + j, LD, stride=64), :
            ].astype(BF16)
        msg[j, :, 1024:1152] = root[pl.ds(j, 16, stride=16), :].astype(BF16)


def tally_kernel(xme, lists, picks, top, counts, sel, top_counts, low, high):
    d = pl.program_id(0)
    x = xme[0]
    codes = lists[0].astype(F32)
    slot_ids = lax.broadcasted_iota(jnp.int32, (256, 256), 0).astype(F32)
    tile_ids = lax.broadcasted_iota(jnp.int32, (TILES, 256), 0).astype(F32)
    for g in range(LD):
        slot_hot = jnp.where(codes[g : g + 1, 0:256] == slot_ids, 1.0, 0.0).astype(BF16)
        tile_hot = jnp.where(codes[g : g + 1, 256:512] == tile_ids, 1.0, 0.0).astype(BF16)
        tally = mm_nt(tile_hot, slot_hot)
        low[pl.ds(g, TILES, stride=LD), :] = tally[:, 0:128]
        high[pl.ds(g, TILES, stride=LD), :] = tally[:, 128:256]
    counts[0, :, 0:128] = low[...].astype(BF16)
    counts[0, :, 128:256] = high[...].astype(BF16)

    @pl.when(d == 0)
    def _():
        lane = lax.broadcasted_iota(jnp.int32, (256, 256), 1)
        for t in range(GROUP):
            hot = jnp.where(picks[:, t : t + 1] == lane, 1.0, 0.0).astype(BF16)
            for s in range(4):
                sel[s, t * 64 : (t + 1) * 64, :] = hot[s * 64 : (s + 1) * 64, :]

    @pl.when(d == 1)
    def _():
        n = top[0:1, :]
        source = top[1:2, :]
        tile = top[2:3, :]
        at = jnp.where(n < 8, n - 4, n - 4)
        m16 = n - 16
        at = jnp.where(n >= 16, jnp.where((m16 & 1) == (x >> 1), 12 + (m16 >> 1), -1), at)
        m32 = n - 32
        at = jnp.where(n >= 32, jnp.where((m32 & 3) == x, 20 + (m32 >> 2), -1), at)
        m64 = n - 64
        at = jnp.where(
            n >= 64,
            jnp.where(((m64 >> 1) & 3) == x, 28 + (m64 >> 3) * 2 + (m64 & 1), -1),
            at,
        )
        code = jnp.where(at >= 0, tile * TARGETS + at, -1)
        width = top.shape[1]
        node = lax.broadcasted_iota(jnp.int32, (128, width), 0)
        source_hot = jnp.where(source == node, 1.0, 0.0).astype(BF16)
        part = 8 * TARGETS
        rows = lax.broadcasted_iota(jnp.int32, (part, width), 0)
        for b in range(8):
            hot = jnp.where(code == rows + b * part, 1.0, 0.0).astype(BF16)
            top_counts[b * part : (b + 1) * part, :] = mm_nt(hot, source_hot).astype(BF16)


def couple_kernel(
    xme, a0, a1, a2, a3, sel, counts, top_counts, table, tt, msg, pool, zs, xtop, acc, root
):
    d = pl.program_id(0)
    x = xme[0]
    blocks = (a0, a1, a2, a3)
    total = 256 + TARGETS

    @pl.when(d == 0)
    def _():
        for s in range(4):
            panels = blocks[s][:, :, 0:LANES].reshape(256, LANES)
            for m in range(4):
                got = mm(sel[s, m * 256 : (m + 1) * 256, :], panels).astype(BF16)
                for t in range(4):
                    pool[m * 4 + t, s * 64 : (s + 1) * 64, :] = got[t * 64 : (t + 1) * 64, :]

    for m in range(4):
        z = mm(counts[0, m * 256 : (m + 1) * 256, :], pool[d]).astype(BF16)
        zs[m * 16 : (m + 1) * 16, d] = z.reshape(16, 16, LANES)

    @pl.when(d == GROUP - 1)
    def _():
        xtop[...] = jnp.zeros_like(xtop)
        for s in range(4):
            for q in range(GROUP):
                n = 64 + (q >> 1) * 8 + ((x - s) & 3) * 2 + (q & 1)
                xtop[pl.ds(n, ROWS, stride=128), :] = blocks[s][q, :, LANES:].astype(F32)[0:ROWS]
        for n in range(63, 3, -1):
            left = xtop[pl.ds(2 * n, ROWS, stride=128), :]
            right = xtop[pl.ds(2 * n + 1, ROWS, stride=128), :]
            pair = jnp.concatenate([left, right], axis=1).astype(BF16)
            up = mm(pair, tt[2 * n - 8 : 2 * n - 6].reshape(2 * RANK, RANK))
            xtop[pl.ds(n, ROWS, stride=128), :] = up.astype(BF16).astype(F32)
        sources = jnp.concatenate(
            [xtop[r * 128 : (r + 1) * 128, :] for r in range(ROWS)], axis=1
        ).astype(BF16)
        part = 8 * TARGETS
        for b in range(8):
            z = mm(top_counts[b * part : (b + 1) * part, :], sources).astype(BF16)
            zs[b * 8 : (b + 1) * 8, 16:19] = z.reshape(8, 3, 16, LANES)
        acc[...] = jnp.zeros_like(acc)

        def step(i, carry):
            for r in range(ROWS):
                lanes = slice(r * RANK, (r + 1) * RANK)
                done = None
                for h in range(2):
                    k = i * 4 + h * 2
                    both = jnp.concatenate(
                        [
                            zs[k, :, :, lanes].reshape(total, RANK),
                            zs[k + 1, :, :, lanes].reshape(total, RANK),
                        ],
                        axis=1,
                    )
                    term = mm(both, table[pl.ds(k, 2)].reshape(2 * RANK, RANK))
                    done = term if done is None else done + term
                acc[r * total : (r + 1) * total, :] += done
            return carry

        lax.fori_loop(0, TILES // 4, step, 0)

        def get(t):
            return acc[pl.ds(256 + t, ROWS, stride=total), :]

        def add(t, value):
            acc[pl.ds(256 + t, ROWS, stride=total), :] += value

        for i in range(4):
            y = mm_nt(get(i).astype(BF16), tt[2 * i : 2 * i + 2].reshape(2 * RANK, RANK))
            add(4 + 2 * i, y[:, 0:RANK])
            add(5 + 2 * i, y[:, RANK:])
        for z in range(8):
            add(12 + z, mm_nt(get(4 + z).astype(BF16), tt[8 + z * 2 + (x >> 1)]))
        for z in range(8):
            add(20 + z, mm_nt(get(12 + z).astype(BF16), tt[24 + z * 4 + x]))
        for z in range(8):
            pair = tt[pl.ds(56 + z * 8 + x * 2, 2)].reshape(2 * RANK, RANK)
            y = mm_nt(get(20 + z).astype(BF16), pair)
            add(28 + 2 * z, y[:, 0:RANK])
            add(29 + 2 * z, y[:, RANK:])
        root[...] = jnp.zeros_like(root)
        for q in range(GROUP):
            for r in range(ROWS):
                msg[q, :, r * RANK : (r + 1) * RANK] = acc[
                    r * total + q * 16 : r * total + (q + 1) * 16, :
                ].astype(BF16)
            root[q * 16 : q * 16 + ROWS, :] = get(28 + q)
            msg[q, :, LANES:] = root[q * 16 : (q + 1) * 16, :].astype(BF16)


def spread_kernel(msg, basis, trans, out, panels, root):
    for j in range(GROUP):
        for r in range(ROWS):
            panels[r * 256 + j * 16 : r * 256 + (j + 1) * 16, :] = msg[
                j, :, r * RANK : (r + 1) * RANK
            ].astype(F32)
        root[pl.ds(j, ROWS, stride=GROUP), :] = msg[j, :, LANES:].astype(F32)[0:ROWS]
    current = [root[...]]
    count = 2
    while count <= LD:
        below = []
        for h in range(count // 2):
            at = count - 2 + 2 * h
            y = mm_nt(current[h].astype(BF16), trans[at : at + 2].reshape(2 * RANK, RANK))
            below += [y[:, 0:RANK], y[:, RANK:]]
        current = below
        count *= 2
    for g in range(LD):
        coupled = jnp.concatenate(
            [panels[pl.ds(r * 256 + g, GROUP, stride=16), :] for r in range(ROWS)], axis=0
        )
        w = (current[g] + coupled).astype(BF16)
        out[:, g * RANK : (g + 1) * RANK] = mm_nt(w, basis[g * RANK : (g + 1) * RANK, :]).astype(
            BF16
        )


SMEM = pl.BlockSpec(memory_space=pltpu.SMEM)
WHOLE = pl.BlockSpec(memory_space=pltpu.VMEM)


def params():
    return pltpu.CompilerParams(vmem_limit_bytes=VMEM_LIMIT)


def fixed(shape):
    return pl.BlockSpec(shape, lambda d: (0,) * len(shape), pipeline_mode=pl.Buffered(1))


def cost(flops, moved):
    return pl.CostEstimate(flops=flops, bytes_accessed=moved, transcendentals=0)


def shards(
    rhs_block,
    leaf_basis,
    local_transfer,
    top_transfer,
    coupling_tiles,
    send_index,
    leaf_list,
    top_list,
):
    x = lax.axis_index("x")
    xme = x.astype(jnp.int32).reshape(1)
    trans = local_transfer.reshape(30, RANK, RANK)
    table = lax.all_gather(coupling_tiles, "rhs", axis=0, tiled=True)
    msg = pl.pallas_call(
        gather_kernel,
        out_shape=jax.ShapeDtypeStruct((GROUP, LD, 1152), BF16),
        in_specs=[SMEM] + [WHOLE] * 4,
        out_specs=WHOLE,
        scratch_shapes=[pltpu.VMEM((1024, RANK), F32), pltpu.VMEM((256, RANK), F32)],
        compiler_params=params(),
        name="leaf_panels",
    )(xme, rhs_block, leaf_basis, trans, leaf_list)
    msg = lax.all_to_all(msg, ("z", "core"), 0, 0, tiled=True)
    mine = msg[:, :, 512:1152]
    blocks = [mine] + [
        lax.ppermute(mine, "x", [(i, (i + s) % 4) for i in range(4)]) for s in (1, 2, 3)
    ]
    index = send_index.reshape(8, 4, 2, 8, 4, 2, 4)
    index = lax.dynamic_index_in_dim(index, x, 4, keepdims=False)
    index = jnp.concatenate(
        [lax.dynamic_slice_in_dim(index, (x - s) % 4, 1, 1) for s in range(4)], axis=1
    )
    index = index.transpose(1, 0, 2, 5, 3, 4)
    place = (jnp.arange(8)[:, None] * 2 + jnp.arange(2)[None, :])[None, :, :, None, None, None]
    picks = jnp.where(index >= 0, index + 16 * place, -1).reshape(256, GROUP).astype(jnp.int32)
    counts, sel, top_counts = pl.pallas_call(
        tally_kernel,
        grid=(GROUP,),
        out_shape=(
            jax.ShapeDtypeStruct((GROUP, 1024, 256), BF16),
            jax.ShapeDtypeStruct((4, 1024, 256), BF16),
            jax.ShapeDtypeStruct((TILES * TARGETS, 128), BF16),
        ),
        in_specs=[
            SMEM,
            pl.BlockSpec((1, LD, 512), lambda d: (d, 0, 0)),
            fixed((256, GROUP)),
            fixed(top_list.shape),
        ],
        out_specs=(
            pl.BlockSpec((1, 1024, 256), lambda d: (d, 0, 0)),
            pl.BlockSpec((4, 1024, 256), lambda d: (0, 0, 0)),
            pl.BlockSpec((TILES * TARGETS, 128), lambda d: (0, 0)),
        ),
        scratch_shapes=[pltpu.VMEM((1024, 128), F32)] * 2,
        compiler_params=params(),
        cost_estimate=cost(4_000_000_000, 12_000_000),
        name="tallies",
    )(xme, msg, picks, top_list)
    total = 256 + TARGETS
    back = pl.pallas_call(
        couple_kernel,
        grid=(GROUP,),
        out_shape=jax.ShapeDtypeStruct((GROUP, LD, 640), BF16),
        in_specs=[SMEM]
        + [fixed((GROUP, LD, 640))] * 4
        + [
            fixed((4, 1024, 256)),
            pl.BlockSpec((1, 1024, 256), lambda d: (d, 0, 0)),
            fixed((TILES * TARGETS, 128)),
            fixed((TILES, RANK, RANK)),
            fixed((120, RANK, RANK)),
        ],
        out_specs=pl.BlockSpec((GROUP, LD, 640), lambda d: (0, 0, 0)),
        scratch_shapes=[
            pltpu.VMEM((GROUP, 256, LANES), BF16),
            pltpu.VMEM((TILES, 19, 16, LANES), BF16),
            pltpu.VMEM((ROWS * 128, RANK), F32),
            pltpu.VMEM((ROWS * total, RANK), F32),
            pltpu.VMEM((GROUP * 16, RANK), F32),
        ],
        compiler_params=params(),
        cost_estimate=cost(8_000_000_000, 20_000_000),
        name="interactions",
    )(xme, *blocks, sel, counts, top_counts, table, top_transfer)
    back = lax.all_to_all(back, ("z", "core"), 0, 0, tiled=True)
    return pl.pallas_call(
        spread_kernel,
        out_shape=jax.ShapeDtypeStruct(rhs_block.shape, BF16),
        in_specs=[WHOLE] * 3,
        out_specs=WHOLE,
        scratch_shapes=[pltpu.VMEM((1024, RANK), F32), pltpu.VMEM((64, RANK), F32)],
        compiler_params=params(),
        name="far_field",
    )(back, leaf_basis, trans)


def solution(mesh):
    grid = Mesh(mesh.devices.reshape(8, 4, 2, 4), ("z", "x", "core", "rhs"))
    leaf = ("z", "x", "core")
    placed = (
        P("rhs", leaf),
        P(leaf, None),
        P(leaf, None, None, None),
        P(),
        P("rhs", None, None),
        P(),
        P(None, leaf, None),
        P(),
    )
    return jax.shard_map(
        shards, mesh=grid, in_specs=placed, out_specs=P("rhs", leaf), check_vma=False
    )
```

```python
import functools

import jax
import jax.numpy as jnp
from jax import lax
from jax.experimental import pallas as pl
from jax.experimental.pallas import tpu as pltpu
from jax.sharding import Mesh, PartitionSpec as P

F32 = jnp.float32
BF16 = jnp.bfloat16
RANK = 128
LD = 16
TILES = 64
ENT = 192
GROUP = 16
ROWS = 4
TARGETS = 48
LANES = ROWS * RANK
DEPTH = 16


def mm(a, b):
    return jnp.dot(a, b, preferred_element_type=F32)


def mm_nt(a, b):
    return lax.dot_general(a, b, (((1,), (1,)), ((), ())), preferred_element_type=F32)


def gather_kernel(xme, rhs, basis, trans, lists, msg, panels, root):
    x = xme[0]
    current = []
    for g in range(LD):
        panel = mm(rhs[:, g * RANK : (g + 1) * RANK], basis[g * RANK : (g + 1) * RANK, :])
        panels[g * 64 : (g + 1) * 64, :] = panel
        current.append(panel.astype(BF16))
    count = LD
    while count > 1:
        above = []
        for h in range(count // 2):
            pair = jnp.concatenate([current[2 * h], current[2 * h + 1]], axis=1)
            at = count - 2 + 2 * h
            above.append(mm(pair, trans[at : at + 2].reshape(2 * RANK, RANK)))
        current = [a.astype(BF16) for a in above]
        count //= 2
    root[...] = jnp.zeros_like(root)
    root[0:64, :] = above[0]
    slot = lists[0]
    p = slot >> 2
    slot = ((x - (p >> 1)) & 3) * 64 + (p >> 3) * 8 + (p & 1) * 4 + (slot & 3)
    slot = slot.astype(F32).astype(BF16)
    tile = lists[1].astype(F32).astype(BF16)
    none = jnp.full((LD, RANK), -1.0, BF16)
    for j in range(GROUP):
        msg[j, :, 128:256] = none
        msg[j, :, 0:192] = slot
        msg[j, :, 384:512] = none
        msg[j, :, 256:448] = tile
        for r in range(ROWS):
            msg[j, :, 512 + r * RANK : 512 + (r + 1) * RANK] = panels[
                pl.ds(r * GROUP + j, LD, stride=64), :
            ].astype(BF16)
        msg[j, :, 1024:1152] = root[pl.ds(j, 16, stride=16), :].astype(BF16)


def choice_kernel(xme, picks, top, sel, top_counts):
    x = xme[0]
    lane = lax.broadcasted_iota(jnp.int32, (256, 256), 1)
    for t in range(GROUP):
        hot = jnp.where(picks[:, t : t + 1] == lane, 1.0, 0.0).astype(BF16)
        for s in range(4):
            sel[s, t * 64 : (t + 1) * 64, :] = hot[s * 64 : (s + 1) * 64, :]
    n = top[0:1, :]
    source = top[1:2, :]
    tile = top[2:3, :]
    m16 = n - 16
    m32 = n - 32
    m64 = n - 64
    at = jnp.where(
        n >= 16, jnp.where((m16 & 1) == (x >> 1), 12 + (m16 >> 1), -1), n - 4
    )
    at = jnp.where(n >= 32, jnp.where((m32 & 3) == x, 20 + (m32 >> 2), -1), at)
    at = jnp.where(
        n >= 64,
        jnp.where(((m64 >> 1) & 3) == x, 28 + (m64 >> 3) * 2 + (m64 & 1), -1),
        at,
    )
    code = jnp.where(at >= 0, tile * TARGETS + at, -1)
    width = top.shape[1]
    node = lax.broadcasted_iota(jnp.int32, (128, width), 0)
    source_hot = jnp.where(source == node, 1.0, 0.0).astype(BF16)
    part = 8 * TARGETS
    rows = lax.broadcasted_iota(jnp.int32, (part, width), 0)
    for b in range(8):
        hot = jnp.where(code == rows + b * part, 1.0, 0.0).astype(BF16)
        top_counts[b * part : (b + 1) * part, :] = mm_nt(hot, source_hot).astype(BF16)


def tally_kernel(lists, counts, low0, high0, low1, high1):
    one = jnp.ones((), BF16)
    zero = jnp.zeros((), BF16)
    low_ids = lax.broadcasted_iota(jnp.int32, (ENT, 128), 1).astype(F32).astype(BF16)
    high_ids = low_ids + 128
    tile_ids = lax.broadcasted_iota(jnp.int32, (TILES, ENT), 0).astype(F32).astype(BF16)

    def settle(low, high, d, g):
        rows = slice(g * TILES, (g + 1) * TILES)
        counts[d, rows, 0:128] = low[rows, :].astype(BF16)
        counts[d, rows, 128:256] = high[rows, :].astype(BF16)

    def device(d, low, high, low_before, high_before):
        codes = lists[d].astype(F32)
        slots = jnp.transpose(codes[:, 0:256])
        tiles = codes[:, 256 : 256 + ENT]
        for g in range(LD):
            slot = jnp.broadcast_to(slots[0:ENT, g : g + 1], (ENT, 128)).astype(BF16)
            slot_hot = jnp.concatenate(
                [jnp.where(slot == low_ids, one, zero), jnp.where(slot == high_ids, one, zero)],
                axis=1,
            )
            tile = tiles[g : g + 1, :].astype(BF16)
            tally = mm(jnp.where(tile == tile_ids, one, zero), slot_hot)
            low[pl.ds(g, TILES, stride=LD), :] = tally[:, 0:128]
            high[pl.ds(g, TILES, stride=LD), :] = tally[:, 128:256]
            settle(low_before, high_before, jnp.maximum(d - 1, 0), g)

    low1[...] = jnp.zeros_like(low1)
    high1[...] = jnp.zeros_like(high1)

    def two(i, carry):
        device(2 * i, low0, high0, low1, high1)
        device(2 * i + 1, low1, high1, low0, high0)
        return carry

    lax.fori_loop(0, GROUP // 2, two, 0)
    for g in range(LD):
        settle(low1, high1, GROUP - 1, g)


def couple_kernel(
    xme,
    yme,
    a0,
    a1,
    a2,
    a3,
    sel,
    counts,
    top_counts,
    t0,
    t1,
    t2,
    t3,
    tt,
    msg,
    pool,
    zs,
    xtop,
    acc,
    root,
):
    x = xme[0]
    total = 256 + TARGETS
    held = (a0, a1, a2, a3)
    xtop[...] = jnp.zeros_like(xtop)
    acc[...] = jnp.zeros_like(acc)
    root[...] = jnp.zeros_like(root)
    for s in range(4):
        panels = held[s][:, :, 0:LANES].reshape(256, LANES)
        for m in range(4):
            got = mm(sel[s, m * 256 : (m + 1) * 256, :], panels).astype(BF16)
            for t in range(4):
                pool[m * 4 + t, s * 64 : (s + 1) * 64, :] = got[t * 64 : (t + 1) * 64, :]

    def device(d, carry):
        for m in range(4):
            z = mm(counts[d, m * 256 : (m + 1) * 256, :], pool[d]).astype(BF16)
            zs[m * 16 : (m + 1) * 16, d] = z.reshape(16, 16, LANES)
        return carry

    lax.fori_loop(0, GROUP, device, 0)
    for s in range(4):
        for q in range(GROUP):
            n = 64 + (q >> 1) * 8 + ((x - s) & 3) * 2 + (q & 1)
            xtop[pl.ds(n, ROWS, stride=128), :] = held[s][q, :, LANES:].astype(F32)[0:ROWS]
    for n in range(63, 3, -1):
        left = xtop[pl.ds(2 * n, ROWS, stride=128), :]
        right = xtop[pl.ds(2 * n + 1, ROWS, stride=128), :]
        pair = jnp.concatenate([left, right], axis=1).astype(BF16)
        up = mm(pair, tt[2 * n - 8 : 2 * n - 6].reshape(2 * RANK, RANK))
        xtop[pl.ds(n, ROWS, stride=128), :] = up.astype(BF16).astype(F32)
    sources = jnp.concatenate(
        [xtop[r * 128 : (r + 1) * 128, :] for r in range(ROWS)], axis=1
    ).astype(BF16)
    part = 8 * TARGETS
    for b in range(8):
        z = mm(top_counts[b * part : (b + 1) * part, :], sources).astype(BF16)
        zs[b * 8 : (b + 1) * 8, 16:19] = z.reshape(8, 3, 16, LANES)

    for y, table in enumerate((t0, t1, t2, t3)):
        first = ((yme[0] - y) & 3) * 16

        def step(i, carry):
            k = i * DEPTH
            tiles = table[pl.ds(k, DEPTH)].reshape(DEPTH * RANK, RANK)
            for r in range(ROWS):
                lanes = slice(r * RANK, (r + 1) * RANK)
                wide = jnp.concatenate(
                    [zs[first + k + h, :, :, lanes].reshape(total, RANK) for h in range(DEPTH)],
                    axis=1,
                )
                acc[r * total : (r + 1) * total, :] += mm(wide, tiles)
            return carry

        lax.fori_loop(0, 16 // DEPTH, step, 0)

    def get(t):
        return acc[pl.ds(256 + t, ROWS, stride=total), :]

    def add(t, value):
        acc[pl.ds(256 + t, ROWS, stride=total), :] += value

    for i in range(4):
        y = mm_nt(get(i).astype(BF16), tt[2 * i : 2 * i + 2].reshape(2 * RANK, RANK))
        add(4 + 2 * i, y[:, 0:RANK])
        add(5 + 2 * i, y[:, RANK:])
    for z in range(8):
        add(12 + z, mm_nt(get(4 + z).astype(BF16), tt[8 + z * 2 + (x >> 1)]))
    for z in range(8):
        add(20 + z, mm_nt(get(12 + z).astype(BF16), tt[24 + z * 4 + x]))
    for z in range(8):
        pair = tt[pl.ds(56 + z * 8 + x * 2, 2)].reshape(2 * RANK, RANK)
        y = mm_nt(get(20 + z).astype(BF16), pair)
        add(28 + 2 * z, y[:, 0:RANK])
        add(29 + 2 * z, y[:, RANK:])
    for q in range(GROUP):
        for r in range(ROWS):
            msg[q, :, r * RANK : (r + 1) * RANK] = acc[
                r * total + q * 16 : r * total + (q + 1) * 16, :
            ].astype(BF16)
        root[q * 16 : q * 16 + ROWS, :] = get(28 + q)
        msg[q, :, LANES:] = root[q * 16 : (q + 1) * 16, :].astype(BF16)


def spread_kernel(msg, basis, trans, out, panels, root):
    for j in range(GROUP):
        for r in range(ROWS):
            panels[r * 256 + j * 16 : r * 256 + (j + 1) * 16, :] = msg[
                j, :, r * RANK : (r + 1) * RANK
            ].astype(F32)
        root[pl.ds(j, ROWS, stride=GROUP), :] = msg[j, :, LANES:].astype(F32)[0:ROWS]
    current = [root[...]]
    count = 2
    while count <= LD:
        below = []
        for h in range(count // 2):
            at = count - 2 + 2 * h
            y = mm_nt(current[h].astype(BF16), trans[at : at + 2].reshape(2 * RANK, RANK))
            below += [y[:, 0:RANK], y[:, RANK:]]
        current = below
        count *= 2
    for g in range(LD):
        coupled = jnp.concatenate(
            [panels[pl.ds(r * 256 + g, GROUP, stride=16), :] for r in range(ROWS)], axis=0
        )
        w = (current[g] + coupled).astype(BF16)
        out[:, g * RANK : (g + 1) * RANK] = mm_nt(w, basis[g * RANK : (g + 1) * RANK, :]).astype(
            BF16
        )


SMEM = pl.BlockSpec(memory_space=pltpu.SMEM)
WHOLE = pl.BlockSpec(memory_space=pltpu.VMEM)


def params(mib):
    return pltpu.CompilerParams(vmem_limit_bytes=mib * 1024 * 1024)


def cost(flops, moved):
    return pl.CostEstimate(flops=flops, bytes_accessed=moved, transcendentals=0)


def shards(
    rhs_block,
    leaf_basis,
    local_transfer,
    top_transfer,
    coupling_tiles,
    send_index,
    leaf_list,
    top_list,
):
    x = lax.axis_index("x")
    xme = x.astype(jnp.int32).reshape(1)
    trans = local_transfer.reshape(30, RANK, RANK)
    yme = lax.axis_index("rhs").astype(jnp.int32).reshape(1)
    tables = [coupling_tiles] + [
        lax.ppermute(coupling_tiles, "rhs", [(i, (i + s) % 4) for i in range(4)])
        for s in (1, 2, 3)
    ]
    msg = pl.pallas_call(
        gather_kernel,
        out_shape=jax.ShapeDtypeStruct((GROUP, LD, 1152), BF16),
        in_specs=[SMEM] + [WHOLE] * 4,
        out_specs=WHOLE,
        scratch_shapes=[pltpu.VMEM((1024, RANK), F32), pltpu.VMEM((256, RANK), F32)],
        compiler_params=params(60),
        name="leaf_panels",
    )(xme, rhs_block, leaf_basis, trans, leaf_list)
    msg = lax.all_to_all(msg, ("z", "core"), 0, 0, tiled=True)
    mine = msg[:, :, 512:1152]
    blocks = [mine] + [
        lax.ppermute(mine, "x", [(i, (i + s) % 4) for i in range(4)]) for s in (1, 2, 3)
    ]
    index = send_index.reshape(8, 4, 2, 8, 4, 2, 4)
    index = lax.dynamic_index_in_dim(index, x, 4, keepdims=False)
    index = jnp.concatenate(
        [lax.dynamic_slice_in_dim(index, (x - s) % 4, 1, 1) for s in range(4)], axis=1
    )
    index = index.transpose(1, 0, 2, 5, 3, 4)
    place = (jnp.arange(8)[:, None] * 2 + jnp.arange(2)[None, :])[None, :, :, None, None, None]
    picks = jnp.where(index >= 0, index + 16 * place, -1).reshape(256, GROUP).astype(jnp.int32)
    sel, top_counts = pl.pallas_call(
        choice_kernel,
        out_shape=(
            jax.ShapeDtypeStruct((4, 1024, 256), BF16),
            jax.ShapeDtypeStruct((TILES * TARGETS, 128), BF16),
        ),
        in_specs=[SMEM] + [WHOLE] * 2,
        out_specs=(WHOLE, WHOLE),
        compiler_params=params(16),
        cost_estimate=cost(400_000_000, 3_000_000),
        name="choices",
    )(xme, picks, top_list)
    counts = pl.pallas_call(
        tally_kernel,
        out_shape=jax.ShapeDtypeStruct((GROUP, 1024, 256), BF16),
        in_specs=[WHOLE],
        out_specs=WHOLE,
        scratch_shapes=[pltpu.VMEM((1024, 128), F32)] * 4,
        compiler_params=params(6),
        cost_estimate=cost(4_000_000_000, 12_000_000),
        name="tallies",
    )(msg)
    total = 256 + TARGETS
    back = pl.pallas_call(
        couple_kernel,
        out_shape=jax.ShapeDtypeStruct((GROUP, LD, 640), BF16),
        in_specs=[SMEM] * 2 + [WHOLE] * 12,
        out_specs=WHOLE,
        scratch_shapes=[
            pltpu.VMEM((GROUP, 256, LANES), BF16),
            pltpu.VMEM((TILES, 19, 16, LANES), BF16),
            pltpu.VMEM((ROWS * 128, RANK), F32),
            pltpu.VMEM((ROWS * total, RANK), F32),
            pltpu.VMEM((GROUP * 16, RANK), F32),
        ],
        compiler_params=params(28),
        cost_estimate=cost(8_000_000_000, 20_000_000),
        name="interactions",
    )(xme, yme, *blocks, sel, counts, top_counts, *tables, top_transfer)
    back = lax.all_to_all(back, ("z", "core"), 0, 0, tiled=True)
    return pl.pallas_call(
        spread_kernel,
        out_shape=jax.ShapeDtypeStruct(rhs_block.shape, BF16),
        in_specs=[WHOLE] * 3,
        out_specs=WHOLE,
        scratch_shapes=[pltpu.VMEM((1024, RANK), F32), pltpu.VMEM((64, RANK), F32)],
        compiler_params=params(8),
        name="far_field",
    )(back, leaf_basis, trans)


def solution(mesh):
    grid = Mesh(mesh.devices.reshape(8, 4, 2, 4), ("z", "x", "core", "rhs"))
    leaf = ("z", "x", "core")
    placed = (
        P("rhs", leaf),
        P(leaf, None),
        P(leaf, None, None, None),
        P(),
        P("rhs", None, None),
        P(),
        P(None, leaf, None),
        P(),
    )
    return jax.shard_map(
        shards, mesh=grid, in_specs=placed, out_specs=P("rhs", leaf), check_vma=False
    )
```

```python
import functools

import jax
import jax.numpy as jnp
from jax import lax
from jax.experimental import pallas as pl
from jax.experimental.pallas import tpu as pltpu
from jax.sharding import Mesh, PartitionSpec as P

F32 = jnp.float32
BF16 = jnp.bfloat16
RANK = 128
LD = 16
TILES = 64
ENT = 192
GROUP = 16
ROWS = 4
TARGETS = 48
LANES = ROWS * RANK
CHUNK = 32
DEPTH = 16


def mm(a, b):
    return jnp.dot(a, b, preferred_element_type=F32)


def mm_nt(a, b):
    return lax.dot_general(a, b, (((1,), (1,)), ((), ())), preferred_element_type=F32)


def gather_kernel(xme, rhs, basis, trans, lists, msg, panels, root):
    x = xme[0]
    current = []
    for g in range(LD):
        panel = mm(rhs[:, g * RANK : (g + 1) * RANK], basis[g * RANK : (g + 1) * RANK, :])
        panels[g * 64 : (g + 1) * 64, :] = panel
        current.append(panel.astype(BF16))
    count = LD
    while count > 1:
        above = []
        for h in range(count // 2):
            pair = jnp.concatenate([current[2 * h], current[2 * h + 1]], axis=1)
            at = count - 2 + 2 * h
            above.append(mm(pair, trans[at : at + 2].reshape(2 * RANK, RANK)))
        current = [a.astype(BF16) for a in above]
        count //= 2
    root[...] = jnp.zeros_like(root)
    root[0:64, :] = above[0]
    slot = lists[0]
    p = slot >> 2
    slot = ((x - (p >> 1)) & 3) * 64 + (p >> 3) * 8 + (p & 1) * 4 + (slot & 3)
    slot = slot.astype(F32)
    tile = lists[1].astype(F32)
    codes = jnp.concatenate([slot, tile], axis=1).astype(BF16)
    for j in range(GROUP):
        msg[j, :, 0 : 2 * ENT] = codes
        msg[j, :, 384:512] = root[pl.ds(j, 16, stride=16), :].astype(BF16)
        for r in range(ROWS):
            msg[j, :, 512 + r * RANK : 512 + (r + 1) * RANK] = panels[
                pl.ds(r * GROUP + j, LD, stride=64), :
            ].astype(BF16)


def pack_kernel(msg, out, root):
    out[0:256, :] = msg[:, :, 512:1024].reshape(256, LANES)
    root[...] = msg[:, :, 384:512].reshape(256, RANK).astype(F32)
    for r in range(ROWS):
        out[256:272, r * RANK : (r + 1) * RANK] = root[pl.ds(r, GROUP, stride=LD), :].astype(BF16)


def choice_kernel(xme, index, top, sel, top_counts, rows):
    x = xme[0]
    for s in range(4):
        for q in range(GROUP):
            p = (q >> 1) * 8 + ((x - s) & 3) * 2 + (q & 1)
            rows[s * 64 + q * 4 : s * 64 + q * 4 + 4, :] = index[p].astype(F32)
    d = lax.broadcasted_iota(jnp.int32, (64, GROUP), 0)
    t = lax.broadcasted_iota(jnp.int32, (64, GROUP), 1)
    mine = jnp.where(d == (t >> 1) * 8 + x * 2 + (t & 1), 1.0, 0.0).astype(BF16)
    picks = mm(rows[...].astype(BF16), mine)
    place = lax.broadcasted_iota(jnp.int32, (256, GROUP), 0)
    picks = jnp.where(picks >= 0, picks + ((place >> 2) & 15).astype(F32) * 16, -1.0)
    lane = lax.broadcasted_iota(jnp.int32, (256, 256), 1).astype(F32)
    for t in range(GROUP):
        hot = jnp.where(picks[:, t : t + 1] == lane, 1.0, 0.0).astype(BF16)
        for s in range(4):
            sel[s, t * 64 : (t + 1) * 64, :] = hot[s * 64 : (s + 1) * 64, :]
    n = top[0:1, :]
    source = top[1:2, :]
    tile = top[2:3, :]
    m16 = n - 16
    m32 = n - 32
    m64 = n - 64
    at = jnp.where(
        n >= 16, jnp.where((m16 & 1) == (x >> 1), 12 + (m16 >> 1), -1), n - 4
    )
    at = jnp.where(n >= 32, jnp.where((m32 & 3) == x, 20 + (m32 >> 2), -1), at)
    at = jnp.where(
        n >= 64,
        jnp.where(((m64 >> 1) & 3) == x, 28 + (m64 >> 3) * 2 + (m64 & 1), -1),
        at,
    )
    code = jnp.where(at >= 0, tile * TARGETS + at, -1)
    width = top.shape[1]
    node = lax.broadcasted_iota(jnp.int32, (128, width), 0)
    source_hot = jnp.where(source == node, 1.0, 0.0).astype(BF16)
    part = 8 * TARGETS
    rows = lax.broadcasted_iota(jnp.int32, (part, width), 0)
    for b in range(8):
        hot = jnp.where(code == rows + b * part, 1.0, 0.0).astype(BF16)
        top_counts[b * part : (b + 1) * part, :] = mm_nt(hot, source_hot).astype(BF16)


def tally_kernel(lists, counts, low0, high0, low1, high1):
    one = jnp.ones((), BF16)
    zero = jnp.zeros((), BF16)
    low_ids = lax.broadcasted_iota(jnp.int32, (ENT, 128), 1).astype(F32).astype(BF16)
    high_ids = low_ids + 128
    tile_ids = lax.broadcasted_iota(jnp.int32, (TILES, ENT), 0).astype(F32).astype(BF16)

    def settle(low, high, d, g):
        rows = slice(g * TILES, (g + 1) * TILES)
        counts[d, rows, 0:128] = low[rows, :].astype(BF16)
        counts[d, rows, 128:256] = high[rows, :].astype(BF16)

    def device(d, low, high, low_before, high_before):
        codes = lists[d].astype(F32)
        slots = jnp.transpose(codes[:, 0:256])
        tiles = codes[:, ENT : 2 * ENT]
        for g in range(LD):
            slot = jnp.broadcast_to(slots[0:ENT, g : g + 1], (ENT, 128)).astype(BF16)
            slot_hot = jnp.concatenate(
                [jnp.where(slot == low_ids, one, zero), jnp.where(slot == high_ids, one, zero)],
                axis=1,
            )
            tile = tiles[g : g + 1, :].astype(BF16)
            tally = mm(jnp.where(tile == tile_ids, one, zero), slot_hot)
            low[pl.ds(g, TILES, stride=LD), :] = tally[:, 0:128]
            high[pl.ds(g, TILES, stride=LD), :] = tally[:, 128:256]
            settle(low_before, high_before, jnp.maximum(d - 1, 0), g)

    low1[...] = jnp.zeros_like(low1)
    high1[...] = jnp.zeros_like(high1)

    def two(i, carry):
        device(2 * i, low0, high0, low1, high1)
        device(2 * i + 1, low1, high1, low0, high0)
        return carry

    lax.fori_loop(0, GROUP // 2, two, 0)
    for g in range(LD):
        settle(low1, high1, GROUP - 1, g)


def couple_kernel(
    xme,
    yme,
    a0,
    a1,
    a2,
    a3,
    sel,
    counts,
    top_counts,
    t0,
    t1,
    t2,
    t3,
    tt,
    msg,
    pool,
    zs,
    xtop,
    acc,
    root,
):
    x = xme[0]
    total = 256 + TARGETS
    held = (a0, a1, a2, a3)
    xtop[...] = jnp.zeros_like(xtop)
    acc[...] = jnp.zeros_like(acc)
    for s in range(4):
        panels = held[s][0:256, :]
        got = mm(sel[s], panels).astype(BF16)
        for t in range(GROUP):
            pool[t, s * 64 : (s + 1) * 64, :] = got[t * 64 : (t + 1) * 64, :]

    def device(d, carry):
        for m in range(TILES // CHUNK):
            z = mm(counts[d, m * CHUNK * 16 : (m + 1) * CHUNK * 16, :], pool[d]).astype(BF16)
            zs[m * CHUNK : (m + 1) * CHUNK, d] = z.reshape(CHUNK, 16, LANES)
        return carry

    lax.fori_loop(0, GROUP, device, 0)
    for s in range(4):
        for r in range(ROWS):
            root[0:GROUP, :] = held[s][256:272, r * RANK : (r + 1) * RANK].astype(F32)
            for z in range(8):
                n = 64 + z * 8 + ((x - s) & 3) * 2
                xtop[pl.ds(r * 128 + n, 2), :] = root[2 * z : 2 * z + 2, :]
    for n in range(63, 3, -1):
        left = xtop[pl.ds(2 * n, ROWS, stride=128), :]
        right = xtop[pl.ds(2 * n + 1, ROWS, stride=128), :]
        pair = jnp.concatenate([left, right], axis=1).astype(BF16)
        up = mm(pair, tt[2 * n - 8 : 2 * n - 6].reshape(2 * RANK, RANK))
        xtop[pl.ds(n, ROWS, stride=128), :] = up.astype(BF16).astype(F32)
    sources = jnp.concatenate(
        [xtop[r * 128 : (r + 1) * 128, :] for r in range(ROWS)], axis=1
    ).astype(BF16)
    part = 8 * TARGETS
    for b in range(8):
        z = mm(top_counts[b * part : (b + 1) * part, :], sources).astype(BF16)
        zs[b * 8 : (b + 1) * 8, 16:19] = z.reshape(8, 3, 16, LANES)

    for y, table in enumerate((t0, t1, t2, t3)):
        first = ((yme[0] - y) & 3) * 16

        def step(i, carry):
            k = i * DEPTH
            tiles = table[pl.ds(k, DEPTH)].reshape(DEPTH * RANK, RANK)
            for r in range(ROWS):
                lanes = slice(r * RANK, (r + 1) * RANK)
                wide = jnp.concatenate(
                    [zs[first + k + h, :, :, lanes].reshape(total, RANK) for h in range(DEPTH)],
                    axis=1,
                )
                acc[r * total : (r + 1) * total, :] += mm(wide, tiles)
            return carry

        lax.fori_loop(0, 16 // DEPTH, step, 0)

    def get(t):
        return acc[pl.ds(256 + t, ROWS, stride=total), :]

    def add(t, value):
        acc[pl.ds(256 + t, ROWS, stride=total), :] += value

    for i in range(4):
        y = mm_nt(get(i).astype(BF16), tt[2 * i : 2 * i + 2].reshape(2 * RANK, RANK))
        add(4 + 2 * i, y[:, 0:RANK])
        add(5 + 2 * i, y[:, RANK:])
    for z in range(8):
        add(12 + z, mm_nt(get(4 + z).astype(BF16), tt[8 + z * 2 + (x >> 1)]))
    for z in range(8):
        add(20 + z, mm_nt(get(12 + z).astype(BF16), tt[24 + z * 4 + x]))
    for z in range(8):
        pair = tt[pl.ds(56 + z * 8 + x * 2, 2)].reshape(2 * RANK, RANK)
        y = mm_nt(get(20 + z).astype(BF16), pair)
        add(28 + 2 * z, y[:, 0:RANK])
        add(29 + 2 * z, y[:, RANK:])
    root[...] = jnp.zeros_like(root)
    for q in range(GROUP):
        for r in range(ROWS):
            msg[q, :, r * RANK : (r + 1) * RANK] = acc[
                r * total + q * 16 : r * total + (q + 1) * 16, :
            ].astype(BF16)
        root[q * 16 : q * 16 + ROWS, :] = get(28 + q)
        msg[q, :, LANES:] = root[q * 16 : (q + 1) * 16, :].astype(BF16)


def spread_kernel(msg, basis, trans, out, panels, root):
    for j in range(GROUP):
        for r in range(ROWS):
            panels[r * 256 + j * 16 : r * 256 + (j + 1) * 16, :] = msg[
                j, :, r * RANK : (r + 1) * RANK
            ].astype(F32)
        root[pl.ds(j, ROWS, stride=GROUP), :] = msg[j, :, LANES:].astype(F32)[0:ROWS]
    current = [root[...]]
    count = 2
    while count <= LD:
        below = []
        for h in range(count // 2):
            at = count - 2 + 2 * h
            y = mm_nt(current[h].astype(BF16), trans[at : at + 2].reshape(2 * RANK, RANK))
            below += [y[:, 0:RANK], y[:, RANK:]]
        current = below
        count *= 2
    for g in range(LD):
        coupled = jnp.concatenate(
            [panels[pl.ds(r * 256 + g, GROUP, stride=16), :] for r in range(ROWS)], axis=0
        )
        w = (current[g] + coupled).astype(BF16)
        out[:, g * RANK : (g + 1) * RANK] = mm_nt(w, basis[g * RANK : (g + 1) * RANK, :]).astype(
            BF16
        )


SMEM = pl.BlockSpec(memory_space=pltpu.SMEM)
WHOLE = pl.BlockSpec(memory_space=pltpu.VMEM)


def params(mib):
    return pltpu.CompilerParams(vmem_limit_bytes=mib * 1024 * 1024)


def cost(flops, moved):
    return pl.CostEstimate(flops=flops, bytes_accessed=moved, transcendentals=0)


def shards(
    rhs_block,
    leaf_basis,
    local_transfer,
    top_transfer,
    coupling_tiles,
    send_index,
    leaf_list,
    top_list,
):
    x = lax.axis_index("x")
    xme = x.astype(jnp.int32).reshape(1)
    trans = local_transfer.reshape(30, RANK, RANK)
    yme = lax.axis_index("rhs").astype(jnp.int32).reshape(1)
    tables = [coupling_tiles] + [
        lax.ppermute(coupling_tiles, "rhs", [(i, (i + s) % 4) for i in range(4)])
        for s in (1, 2, 3)
    ]
    msg = pl.pallas_call(
        gather_kernel,
        out_shape=jax.ShapeDtypeStruct((GROUP, LD, 1024), BF16),
        in_specs=[SMEM] + [WHOLE] * 4,
        out_specs=WHOLE,
        scratch_shapes=[pltpu.VMEM((1024, RANK), F32), pltpu.VMEM((256, RANK), F32)],
        compiler_params=params(60),
        name="leaf_panels",
    )(xme, rhs_block, leaf_basis, trans, leaf_list)
    msg = lax.all_to_all(msg, ("z", "core"), 0, 0, tiled=True)
    mine = pl.pallas_call(
        pack_kernel,
        out_shape=jax.ShapeDtypeStruct((272, LANES), BF16),
        in_specs=[WHOLE],
        out_specs=WHOLE,
        scratch_shapes=[pltpu.VMEM((256, RANK), F32)],
        compiler_params=params(4),
        name="pack",
    )(msg)
    blocks = [mine] + [
        lax.ppermute(mine, "x", [(i, (i + s) % 4) for i in range(4)]) for s in (1, 2, 3)
    ]
    sel, top_counts = pl.pallas_call(
        choice_kernel,
        out_shape=(
            jax.ShapeDtypeStruct((4, 1024, 256), BF16),
            jax.ShapeDtypeStruct((TILES * TARGETS, 128), BF16),
        ),
        in_specs=[SMEM] + [WHOLE] * 2,
        out_specs=(WHOLE, WHOLE),
        scratch_shapes=[pltpu.VMEM((256, 64), F32)],
        compiler_params=params(56),
        cost_estimate=cost(400_000_000, 3_000_000),
        name="choices",
    )(xme, send_index.transpose(0, 2, 1), top_list)
    counts = pl.pallas_call(
        tally_kernel,
        out_shape=jax.ShapeDtypeStruct((GROUP, 1024, 256), BF16),
        in_specs=[WHOLE],
        out_specs=WHOLE,
        scratch_shapes=[pltpu.VMEM((1024, 128), F32)] * 4,
        compiler_params=params(6),
        cost_estimate=cost(4_000_000_000, 12_000_000),
        name="tallies",
    )(msg)
    total = 256 + TARGETS
    back = pl.pallas_call(
        couple_kernel,
        out_shape=jax.ShapeDtypeStruct((GROUP, LD, 640), BF16),
        in_specs=[SMEM] * 2 + [WHOLE] * 12,
        out_specs=WHOLE,
        scratch_shapes=[
            pltpu.VMEM((GROUP, 256, LANES), BF16),
            pltpu.VMEM((TILES, 19, 16, LANES), BF16),
            pltpu.VMEM((ROWS * 128, RANK), F32),
            pltpu.VMEM((ROWS * total, RANK), F32),
            pltpu.VMEM((GROUP * 16, RANK), F32),
        ],
        compiler_params=params(28),
        cost_estimate=cost(8_000_000_000, 20_000_000),
        name="interactions",
    )(xme, yme, *blocks, sel, counts, top_counts, *tables, top_transfer)
    back = lax.all_to_all(back, ("z", "core"), 0, 0, tiled=True)
    return pl.pallas_call(
        spread_kernel,
        out_shape=jax.ShapeDtypeStruct(rhs_block.shape, BF16),
        in_specs=[WHOLE] * 3,
        out_specs=WHOLE,
        scratch_shapes=[pltpu.VMEM((1024, RANK), F32), pltpu.VMEM((64, RANK), F32)],
        compiler_params=params(8),
        name="far_field",
    )(back, leaf_basis, trans)


def solution(mesh):
    grid = Mesh(mesh.devices.reshape(8, 4, 2, 4), ("z", "x", "core", "rhs"))
    leaf = ("z", "x", "core")
    placed = (
        P("rhs", leaf),
        P(leaf, None),
        P(leaf, None, None, None),
        P(),
        P("rhs", None, None),
        P(),
        P(None, leaf, None),
        P(),
    )
    return jax.shard_map(
        shards, mesh=grid, in_specs=placed, out_specs=P("rhs", leaf), check_vma=False
    )
```

```python
import functools

import jax
import jax.numpy as jnp
from jax import lax
from jax.experimental import pallas as pl
from jax.experimental.pallas import tpu as pltpu
from jax.sharding import Mesh, PartitionSpec as P

F32 = jnp.float32
BF16 = jnp.bfloat16
RANK = 128
LD = 16
TILES = 64
ENT = 192
GROUP = 16
ROWS = 4
TARGETS = 48
LANES = ROWS * RANK
CHUNK = 32
DEPTH = 16


def mm(a, b):
    return jnp.dot(a, b, preferred_element_type=F32)


def mm_nt(a, b):
    return lax.dot_general(a, b, (((1,), (1,)), ((), ())), preferred_element_type=F32)


def gather_kernel(xme, rhs, basis, trans, lists, msg, panels, root):
    x = xme[0]
    current = []
    for g in range(LD):
        panel = mm(rhs[:, g * RANK : (g + 1) * RANK], basis[g * RANK : (g + 1) * RANK, :])
        panels[g * 64 : (g + 1) * 64, :] = panel
        current.append(panel.astype(BF16))
    count = LD
    while count > 1:
        above = []
        for h in range(count // 2):
            pair = jnp.concatenate([current[2 * h], current[2 * h + 1]], axis=1)
            at = count - 2 + 2 * h
            above.append(mm(pair, trans[at : at + 2].reshape(2 * RANK, RANK)))
        current = [a.astype(BF16) for a in above]
        count //= 2
    root[...] = jnp.zeros_like(root)
    root[0:64, :] = above[0]
    slot = lists[0]
    p = slot >> 2
    slot = ((x - (p >> 1)) & 3) * 64 + (p >> 3) * 8 + (p & 1) * 4 + (slot & 3)
    slot = slot.astype(F32)
    tile = lists[1].astype(F32)
    codes = jnp.concatenate([slot, tile], axis=1).astype(BF16)
    for j in range(GROUP):
        msg[j, :, 0 : 2 * ENT] = codes
        msg[j, :, 384:512] = root[pl.ds(j, 16, stride=16), :].astype(BF16)
        for r in range(ROWS):
            msg[j, :, 512 + r * RANK : 512 + (r + 1) * RANK] = panels[
                pl.ds(r * GROUP + j, LD, stride=64), :
            ].astype(BF16)


def pack_kernel(msg, out, root):
    out[0:256, :] = msg[:, :, 512:1024].reshape(256, LANES)
    root[...] = msg[:, :, 384:512].reshape(256, RANK).astype(F32)
    for r in range(ROWS):
        out[256:272, r * RANK : (r + 1) * RANK] = root[pl.ds(r, GROUP, stride=LD), :].astype(BF16)


def choice_kernel(xme, index, top, sel, top_counts, rows):
    x = xme[0]
    for s in range(4):
        for q in range(GROUP):
            p = (q >> 1) * 8 + ((x - s) & 3) * 2 + (q & 1)
            rows[s * 64 + q * 4 : s * 64 + q * 4 + 4, :] = index[p].astype(F32)
    d = lax.broadcasted_iota(jnp.int32, (64, GROUP), 0)
    t = lax.broadcasted_iota(jnp.int32, (64, GROUP), 1)
    mine = jnp.where(d == (t >> 1) * 8 + x * 2 + (t & 1), 1.0, 0.0).astype(BF16)
    picks = mm(rows[...].astype(BF16), mine)
    place = lax.broadcasted_iota(jnp.int32, (256, GROUP), 0)
    picks = jnp.where(picks >= 0, picks + ((place >> 2) & 15).astype(F32) * 16, -1.0)
    lane = lax.broadcasted_iota(jnp.int32, (256, 256), 1).astype(F32)
    for t in range(GROUP):
        hot = jnp.where(picks[:, t : t + 1] == lane, 1.0, 0.0).astype(BF16)
        for s in range(4):
            sel[s, t * 64 : (t + 1) * 64, :] = hot[s * 64 : (s + 1) * 64, :]
    n = top[0:1, :]
    source = top[1:2, :]
    tile = top[2:3, :]
    m16 = n - 16
    m32 = n - 32
    m64 = n - 64
    at = jnp.where(
        n >= 16, jnp.where((m16 & 1) == (x >> 1), 12 + (m16 >> 1), -1), n - 4
    )
    at = jnp.where(n >= 32, jnp.where((m32 & 3) == x, 20 + (m32 >> 2), -1), at)
    at = jnp.where(
        n >= 64,
        jnp.where(((m64 >> 1) & 3) == x, 28 + (m64 >> 3) * 2 + (m64 & 1), -1),
        at,
    )
    code = jnp.where(at >= 0, tile * TARGETS + at, -1)
    width = top.shape[1]
    node = lax.broadcasted_iota(jnp.int32, (128, width), 0)
    source_hot = jnp.where(source == node, 1.0, 0.0).astype(BF16)
    part = 8 * TARGETS
    rows = lax.broadcasted_iota(jnp.int32, (part, width), 0)
    for b in range(8):
        hot = jnp.where(code == rows + b * part, 1.0, 0.0).astype(BF16)
        top_counts[b * part : (b + 1) * part, :] = mm_nt(hot, source_hot).astype(BF16)


def tally_kernel(lists, counts, low0, high0, low1, high1):
    one = jnp.ones((), BF16)
    zero = jnp.zeros((), BF16)
    low_ids = lax.broadcasted_iota(jnp.int32, (ENT, 128), 1).astype(F32).astype(BF16)
    high_ids = low_ids + 128
    tile_ids = lax.broadcasted_iota(jnp.int32, (TILES, ENT), 0).astype(F32).astype(BF16)

    def settle(low, high, d, g):
        rows = slice(g * TILES, (g + 1) * TILES)
        counts[d, rows, 0:128] = low[rows, :].astype(BF16)
        counts[d, rows, 128:256] = high[rows, :].astype(BF16)

    def device(d, low, high, low_before, high_before):
        codes = lists[d].astype(F32)
        slots = jnp.transpose(codes[:, 0:256])
        tiles = codes[:, ENT : 2 * ENT]
        for g in range(LD):
            slot = jnp.broadcast_to(slots[0:ENT, g : g + 1], (ENT, 128)).astype(BF16)
            slot_hot = jnp.concatenate(
                [jnp.where(slot == low_ids, one, zero), jnp.where(slot == high_ids, one, zero)],
                axis=1,
            )
            tile = tiles[g : g + 1, :].astype(BF16)
            tally = mm(jnp.where(tile == tile_ids, one, zero), slot_hot)
            low[pl.ds(g, TILES, stride=LD), :] = tally[:, 0:128]
            high[pl.ds(g, TILES, stride=LD), :] = tally[:, 128:256]
            settle(low_before, high_before, jnp.maximum(d - 1, 0), g)

    low1[...] = jnp.zeros_like(low1)
    high1[...] = jnp.zeros_like(high1)

    def two(i, carry):
        device(2 * i, low0, high0, low1, high1)
        device(2 * i + 1, low1, high1, low0, high0)
        return carry

    lax.fori_loop(0, GROUP // 2, two, 0)
    for g in range(LD):
        settle(low1, high1, GROUP - 1, g)


def couple_kernel(
    xme,
    yme,
    a0,
    a1,
    a2,
    a3,
    sel,
    counts,
    top_counts,
    t0,
    t1,
    t2,
    t3,
    tt,
    msg,
    pool,
    zs,
    xtop,
    acc,
    root,
):
    x = xme[0]
    total = 256 + TARGETS
    held = (a0, a1, a2, a3)
    xtop[...] = jnp.zeros_like(xtop)
    acc[...] = jnp.zeros_like(acc)
    for s in range(4):
        panels = held[s][0:256, :]
        got = mm(sel[s], panels).astype(BF16)
        for t in range(GROUP):
            pool[t, s * 64 : (s + 1) * 64, :] = got[t * 64 : (t + 1) * 64, :]

    def device(d, carry):
        for m in range(TILES // CHUNK):
            z = mm(counts[d, m * CHUNK * 16 : (m + 1) * CHUNK * 16, :], pool[d]).astype(BF16)
            zs[m * CHUNK : (m + 1) * CHUNK, d] = z.reshape(CHUNK, 16, LANES)
        return carry

    lax.fori_loop(0, GROUP, device, 0)
    for s in range(4):
        for r in range(ROWS):
            root[0:GROUP, :] = held[s][256:272, r * RANK : (r + 1) * RANK].astype(F32)
            for z in range(8):
                n = 64 + z * 8 + ((x - s) & 3) * 2
                xtop[pl.ds(r * 128 + n, 2), :] = root[2 * z : 2 * z + 2, :]
    for n in range(63, 3, -1):
        left = xtop[pl.ds(2 * n, ROWS, stride=128), :]
        right = xtop[pl.ds(2 * n + 1, ROWS, stride=128), :]
        pair = jnp.concatenate([left, right], axis=1).astype(BF16)
        up = mm(pair, tt[2 * n - 8 : 2 * n - 6].reshape(2 * RANK, RANK))
        xtop[pl.ds(n, ROWS, stride=128), :] = up.astype(BF16).astype(F32)
    sources = jnp.concatenate(
        [xtop[r * 128 : (r + 1) * 128, :] for r in range(ROWS)], axis=1
    ).astype(BF16)
    part = 8 * TARGETS
    for b in range(8):
        z = mm(top_counts[b * part : (b + 1) * part, :], sources).astype(BF16)
        zs[b * 8 : (b + 1) * 8, 16:19] = z.reshape(8, 3, 16, LANES)

    for y, table in enumerate((t0, t1, t2, t3)):
        first = (yme[0] ^ y) * 16

        def step(i, carry):
            k = i * DEPTH
            tiles = table[pl.ds(k, DEPTH)].reshape(DEPTH * RANK, RANK)
            for r in range(ROWS):
                lanes = slice(r * RANK, (r + 1) * RANK)
                wide = jnp.concatenate(
                    [zs[first + k + h, :, :, lanes].reshape(total, RANK) for h in range(DEPTH)],
                    axis=1,
                )
                acc[r * total : (r + 1) * total, :] += mm(wide, tiles)
            return carry

        lax.fori_loop(0, 16 // DEPTH, step, 0)

    def get(t):
        return acc[pl.ds(256 + t, ROWS, stride=total), :]

    def add(t, value):
        acc[pl.ds(256 + t, ROWS, stride=total), :] += value

    for i in range(4):
        y = mm_nt(get(i).astype(BF16), tt[2 * i : 2 * i + 2].reshape(2 * RANK, RANK))
        add(4 + 2 * i, y[:, 0:RANK])
        add(5 + 2 * i, y[:, RANK:])
    for z in range(8):
        add(12 + z, mm_nt(get(4 + z).astype(BF16), tt[8 + z * 2 + (x >> 1)]))
    for z in range(8):
        add(20 + z, mm_nt(get(12 + z).astype(BF16), tt[24 + z * 4 + x]))
    for z in range(8):
        pair = tt[pl.ds(56 + z * 8 + x * 2, 2)].reshape(2 * RANK, RANK)
        y = mm_nt(get(20 + z).astype(BF16), pair)
        add(28 + 2 * z, y[:, 0:RANK])
        add(29 + 2 * z, y[:, RANK:])
    root[...] = jnp.zeros_like(root)
    for q in range(GROUP):
        for r in range(ROWS):
            msg[q, :, r * RANK : (r + 1) * RANK] = acc[
                r * total + q * 16 : r * total + (q + 1) * 16, :
            ].astype(BF16)
        root[q * 16 : q * 16 + ROWS, :] = get(28 + q)
        msg[q, :, LANES:] = root[q * 16 : (q + 1) * 16, :].astype(BF16)


def spread_kernel(msg, basis, trans, out, panels, root):
    for j in range(GROUP):
        for r in range(ROWS):
            panels[r * 256 + j * 16 : r * 256 + (j + 1) * 16, :] = msg[
                j, :, r * RANK : (r + 1) * RANK
            ].astype(F32)
        root[pl.ds(j, ROWS, stride=GROUP), :] = msg[j, :, LANES:].astype(F32)[0:ROWS]
    current = [root[...]]
    count = 2
    while count <= LD:
        below = []
        for h in range(count // 2):
            at = count - 2 + 2 * h
            y = mm_nt(current[h].astype(BF16), trans[at : at + 2].reshape(2 * RANK, RANK))
            below += [y[:, 0:RANK], y[:, RANK:]]
        current = below
        count *= 2
    for g in range(LD):
        coupled = jnp.concatenate(
            [panels[pl.ds(r * 256 + g, GROUP, stride=16), :] for r in range(ROWS)], axis=0
        )
        w = (current[g] + coupled).astype(BF16)
        out[:, g * RANK : (g + 1) * RANK] = mm_nt(w, basis[g * RANK : (g + 1) * RANK, :]).astype(
            BF16
        )


SMEM = pl.BlockSpec(memory_space=pltpu.SMEM)
WHOLE = pl.BlockSpec(memory_space=pltpu.VMEM)


def params(mib):
    return pltpu.CompilerParams(vmem_limit_bytes=mib * 1024 * 1024)


def cost(flops, moved):
    return pl.CostEstimate(flops=flops, bytes_accessed=moved, transcendentals=0)


def shards(
    rhs_block,
    leaf_basis,
    local_transfer,
    top_transfer,
    coupling_tiles,
    send_index,
    leaf_list,
    top_list,
):
    x = lax.axis_index("x")
    xme = x.astype(jnp.int32).reshape(1)
    trans = local_transfer.reshape(30, RANK, RANK)
    yme = lax.axis_index("rhs").astype(jnp.int32).reshape(1)
    near = lax.ppermute(coupling_tiles, "rhs", [(i, i ^ 1) for i in range(4)])
    over = lax.ppermute(coupling_tiles, "rhs", [(i, i ^ 3) for i in range(4)])
    msg = pl.pallas_call(
        gather_kernel,
        out_shape=jax.ShapeDtypeStruct((GROUP, LD, 1024), BF16),
        in_specs=[SMEM] + [WHOLE] * 4,
        out_specs=WHOLE,
        scratch_shapes=[pltpu.VMEM((1024, RANK), F32), pltpu.VMEM((256, RANK), F32)],
        compiler_params=params(60),
        name="leaf_panels",
    )(xme, rhs_block, leaf_basis, trans, leaf_list)
    msg = lax.all_to_all(msg, ("z", "core"), 0, 0, tiled=True)
    mine = pl.pallas_call(
        pack_kernel,
        out_shape=jax.ShapeDtypeStruct((272, LANES), BF16),
        in_specs=[WHOLE],
        out_specs=WHOLE,
        scratch_shapes=[pltpu.VMEM((256, RANK), F32)],
        compiler_params=params(4),
        name="pack",
    )(msg)
    blocks = [mine] + [
        lax.ppermute(mine, "x", [(i, (i + s) % 4) for i in range(4)]) for s in (1, 2, 3)
    ]
    sel, top_counts = pl.pallas_call(
        choice_kernel,
        out_shape=(
            jax.ShapeDtypeStruct((4, 1024, 256), BF16),
            jax.ShapeDtypeStruct((TILES * TARGETS, 128), BF16),
        ),
        in_specs=[SMEM] + [WHOLE] * 2,
        out_specs=(WHOLE, WHOLE),
        scratch_shapes=[pltpu.VMEM((256, 64), F32)],
        compiler_params=params(56),
        cost_estimate=cost(400_000_000, 3_000_000),
        name="choices",
    )(xme, send_index.transpose(0, 2, 1), top_list)
    near, top_counts = lax.optimization_barrier((near, top_counts))
    across = lax.ppermute(near, "rhs", [(i, i ^ 3) for i in range(4)])
    tables = (coupling_tiles, near, across, over)
    counts = pl.pallas_call(
        tally_kernel,
        out_shape=jax.ShapeDtypeStruct((GROUP, 1024, 256), BF16),
        in_specs=[WHOLE],
        out_specs=WHOLE,
        scratch_shapes=[pltpu.VMEM((1024, 128), F32)] * 4,
        compiler_params=params(6),
        cost_estimate=cost(4_000_000_000, 12_000_000),
        name="tallies",
    )(msg)
    total = 256 + TARGETS
    back = pl.pallas_call(
        couple_kernel,
        out_shape=jax.ShapeDtypeStruct((GROUP, LD, 640), BF16),
        in_specs=[SMEM] * 2 + [WHOLE] * 12,
        out_specs=WHOLE,
        scratch_shapes=[
            pltpu.VMEM((GROUP, 256, LANES), BF16),
            pltpu.VMEM((TILES, 19, 16, LANES), BF16),
            pltpu.VMEM((ROWS * 128, RANK), F32),
            pltpu.VMEM((ROWS * total, RANK), F32),
            pltpu.VMEM((GROUP * 16, RANK), F32),
        ],
        compiler_params=params(28),
        cost_estimate=cost(8_000_000_000, 20_000_000),
        name="interactions",
    )(xme, yme, *blocks, sel, counts, top_counts, *tables, top_transfer)
    back = lax.all_to_all(back, ("z", "core"), 0, 0, tiled=True)
    return pl.pallas_call(
        spread_kernel,
        out_shape=jax.ShapeDtypeStruct(rhs_block.shape, BF16),
        in_specs=[WHOLE] * 3,
        out_specs=WHOLE,
        scratch_shapes=[pltpu.VMEM((1024, RANK), F32), pltpu.VMEM((64, RANK), F32)],
        compiler_params=params(8),
        name="far_field",
    )(back, leaf_basis, trans)


def solution(mesh):
    grid = Mesh(mesh.devices.reshape(8, 4, 2, 4), ("z", "x", "core", "rhs"))
    leaf = ("z", "x", "core")
    placed = (
        P("rhs", leaf),
        P(leaf, None),
        P(leaf, None, None, None),
        P(),
        P("rhs", None, None),
        P(),
        P(None, leaf, None),
        P(),
    )
    return jax.shard_map(
        shards, mesh=grid, in_specs=placed, out_specs=P("rhs", leaf), check_vma=False
    )
```

```python
import functools

import jax
import jax.numpy as jnp
from jax import lax
from jax.experimental import pallas as pl
from jax.experimental.pallas import tpu as pltpu
from jax.sharding import Mesh, PartitionSpec as P

F32 = jnp.float32
BF16 = jnp.bfloat16
RANK = 128
LD = 16
TILES = 64
ENT = 192
GROUP = 16
ROWS = 4
TARGETS = 48
LANES = ROWS * RANK
CHUNK = 32
DEPTH = 16


def mm(a, b):
    return jnp.dot(a, b, preferred_element_type=F32)


def mm_nt(a, b):
    return lax.dot_general(a, b, (((1,), (1,)), ((), ())), preferred_element_type=F32)


def gather_kernel(xme, rhs, basis, trans, lists, msg, panels, root):
    x = xme[0]
    current = []
    for g in range(LD):
        panel = mm(rhs[:, g * RANK : (g + 1) * RANK], basis[g * RANK : (g + 1) * RANK, :])
        panels[g * 64 : (g + 1) * 64, :] = panel
        current.append(panel.astype(BF16))
    count = LD
    while count > 1:
        above = []
        for h in range(count // 2):
            pair = jnp.concatenate([current[2 * h], current[2 * h + 1]], axis=1)
            at = count - 2 + 2 * h
            above.append(mm(pair, trans[at : at + 2].reshape(2 * RANK, RANK)))
        current = [a.astype(BF16) for a in above]
        count //= 2
    root[...] = jnp.zeros_like(root)
    root[0:64, :] = above[0]
    slot = lists[0]
    p = slot >> 2
    slot = ((x - (p >> 1)) & 3) * 64 + (p >> 3) * 8 + (p & 1) * 4 + (slot & 3)
    slot = slot.astype(F32)
    tile = lists[1].astype(F32)
    codes = jnp.concatenate([slot, tile], axis=1).astype(BF16)
    for j in range(GROUP):
        msg[j, :, 0 : 2 * ENT] = codes
        msg[j, :, 384:512] = root[pl.ds(j, 16, stride=16), :].astype(BF16)
        for r in range(ROWS):
            msg[j, :, 512 + r * RANK : 512 + (r + 1) * RANK] = panels[
                pl.ds(r * GROUP + j, LD, stride=64), :
            ].astype(BF16)


def pack_kernel(msg, out, root):
    out[0:256, :] = msg[:, :, 512:1024].reshape(256, LANES)
    root[...] = msg[:, :, 384:512].reshape(256, RANK).astype(F32)
    for r in range(ROWS):
        out[256:272, r * RANK : (r + 1) * RANK] = root[pl.ds(r, GROUP, stride=LD), :].astype(BF16)


def choice_kernel(xme, index, top, sel, top_counts, rows):
    x = xme[0]
    for s in range(4):
        for q in range(GROUP):
            p = (q >> 1) * 8 + ((x - s) & 3) * 2 + (q & 1)
            rows[s * 64 + q * 4 : s * 64 + q * 4 + 4, :] = index[p].astype(F32)
    d = lax.broadcasted_iota(jnp.int32, (64, GROUP), 0)
    t = lax.broadcasted_iota(jnp.int32, (64, GROUP), 1)
    mine = jnp.where(d == (t >> 1) * 8 + x * 2 + (t & 1), 1.0, 0.0).astype(BF16)
    picks = mm(rows[...].astype(BF16), mine)
    place = lax.broadcasted_iota(jnp.int32, (256, GROUP), 0)
    picks = jnp.where(picks >= 0, picks + ((place >> 2) & 15).astype(F32) * 16, -1.0)
    lane = lax.broadcasted_iota(jnp.int32, (256, 256), 1).astype(F32)
    for t in range(GROUP):
        hot = jnp.where(picks[:, t : t + 1] == lane, 1.0, 0.0).astype(BF16)
        for s in range(4):
            sel[s, t * 64 : (t + 1) * 64, :] = hot[s * 64 : (s + 1) * 64, :]
    n = top[0:1, :]
    source = top[1:2, :]
    tile = top[2:3, :]
    m16 = n - 16
    m32 = n - 32
    m64 = n - 64
    at = jnp.where(
        n >= 16, jnp.where((m16 & 1) == (x >> 1), 12 + (m16 >> 1), -1), n - 4
    )
    at = jnp.where(n >= 32, jnp.where((m32 & 3) == x, 20 + (m32 >> 2), -1), at)
    at = jnp.where(
        n >= 64,
        jnp.where(((m64 >> 1) & 3) == x, 28 + (m64 >> 3) * 2 + (m64 & 1), -1),
        at,
    )
    code = jnp.where(at >= 0, tile * TARGETS + at, -1)
    width = top.shape[1]
    node = lax.broadcasted_iota(jnp.int32, (128, width), 0)
    source_hot = jnp.where(source == node, 1.0, 0.0).astype(BF16)
    part = 8 * TARGETS
    rows = lax.broadcasted_iota(jnp.int32, (part, width), 0)
    for b in range(8):
        hot = jnp.where(code == rows + b * part, 1.0, 0.0).astype(BF16)
        top_counts[b * part : (b + 1) * part, :] = mm_nt(hot, source_hot).astype(BF16)


def tally_kernel(lists, counts, low0, high0, low1, high1):
    one = jnp.ones((), BF16)
    zero = jnp.zeros((), BF16)
    low_ids = lax.broadcasted_iota(jnp.int32, (ENT, 128), 1).astype(F32).astype(BF16)
    high_ids = low_ids + 128
    tile_ids = lax.broadcasted_iota(jnp.int32, (TILES, ENT), 0).astype(F32).astype(BF16)

    def settle(low, high, d, g):
        rows = slice(g * TILES, (g + 1) * TILES)
        counts[d, rows, 0:128] = low[rows, :].astype(BF16)
        counts[d, rows, 128:256] = high[rows, :].astype(BF16)

    def device(d, low, high, low_before, high_before):
        codes = lists[d].astype(F32)
        slots = jnp.transpose(codes[:, 0:256])
        tiles = codes[:, ENT : 2 * ENT]
        for g in range(LD):
            slot = jnp.broadcast_to(slots[0:ENT, g : g + 1], (ENT, 128)).astype(BF16)
            slot_hot = jnp.concatenate(
                [jnp.where(slot == low_ids, one, zero), jnp.where(slot == high_ids, one, zero)],
                axis=1,
            )
            tile = tiles[g : g + 1, :].astype(BF16)
            tally = mm(jnp.where(tile == tile_ids, one, zero), slot_hot)
            low[pl.ds(g, TILES, stride=LD), :] = tally[:, 0:128]
            high[pl.ds(g, TILES, stride=LD), :] = tally[:, 128:256]
            settle(low_before, high_before, jnp.maximum(d - 1, 0), g)

    low1[...] = jnp.zeros_like(low1)
    high1[...] = jnp.zeros_like(high1)

    def two(i, carry):
        device(2 * i, low0, high0, low1, high1)
        device(2 * i + 1, low1, high1, low0, high0)
        return carry

    lax.fori_loop(0, GROUP // 2, two, 0)
    for g in range(LD):
        settle(low1, high1, GROUP - 1, g)


def couple_kernel(
    xme,
    yme,
    a0,
    a1,
    a2,
    a3,
    sel,
    counts,
    top_counts,
    t0,
    t1,
    t2,
    t3,
    tt,
    msg,
    pool,
    zs,
    xtop,
    acc,
    root,
):
    x = xme[0]
    total = 256 + TARGETS
    held = (a0, a1, a2, a3)
    xtop[...] = jnp.zeros_like(xtop)
    acc[...] = jnp.zeros_like(acc)
    for s in range(4):
        panels = held[s][0:256, :]
        got = mm(sel[s], panels).astype(BF16)
        for t in range(GROUP):
            pool[t, s * 64 : (s + 1) * 64, :] = got[t * 64 : (t + 1) * 64, :]

    def device(d, carry):
        for m in range(TILES // CHUNK):
            z = mm(counts[d, m * CHUNK * 16 : (m + 1) * CHUNK * 16, :], pool[d]).astype(BF16)
            zs[m * CHUNK : (m + 1) * CHUNK, d] = z.reshape(CHUNK, 16, LANES)
        return carry

    lax.fori_loop(0, GROUP, device, 0, unroll=2)
    for s in range(4):
        for r in range(ROWS):
            root[0:GROUP, :] = held[s][256:272, r * RANK : (r + 1) * RANK].astype(F32)
            for z in range(8):
                n = 64 + z * 8 + ((x - s) & 3) * 2
                xtop[pl.ds(r * 128 + n, 2), :] = root[2 * z : 2 * z + 2, :]
    for n in range(63, 3, -1):
        left = xtop[pl.ds(2 * n, ROWS, stride=128), :]
        right = xtop[pl.ds(2 * n + 1, ROWS, stride=128), :]
        pair = jnp.concatenate([left, right], axis=1).astype(BF16)
        up = mm(pair, tt[2 * n - 8 : 2 * n - 6].reshape(2 * RANK, RANK))
        xtop[pl.ds(n, ROWS, stride=128), :] = up.astype(BF16).astype(F32)
    sources = jnp.concatenate(
        [xtop[r * 128 : (r + 1) * 128, :] for r in range(ROWS)], axis=1
    ).astype(BF16)
    part = 8 * TARGETS
    for b in range(8):
        z = mm(top_counts[b * part : (b + 1) * part, :], sources).astype(BF16)
        zs[b * 8 : (b + 1) * 8, 16:19] = z.reshape(8, 3, 16, LANES)

    for y, table in enumerate((t0, t1, t2, t3)):
        first = (yme[0] ^ y) * 16

        def step(i, carry):
            k = i * DEPTH
            tiles = table[pl.ds(k, DEPTH)].reshape(DEPTH * RANK, RANK)
            for r in range(ROWS):
                lanes = slice(r * RANK, (r + 1) * RANK)
                wide = jnp.concatenate(
                    [zs[first + k + h, :, :, lanes].reshape(total, RANK) for h in range(DEPTH)],
                    axis=1,
                )
                acc[r * total : (r + 1) * total, :] += mm(wide, tiles)
            return carry

        lax.fori_loop(0, 16 // DEPTH, step, 0)

    def get(t):
        return acc[pl.ds(256 + t, ROWS, stride=total), :]

    def add(t, value):
        acc[pl.ds(256 + t, ROWS, stride=total), :] += value

    for i in range(4):
        y = mm_nt(get(i).astype(BF16), tt[2 * i : 2 * i + 2].reshape(2 * RANK, RANK))
        add(4 + 2 * i, y[:, 0:RANK])
        add(5 + 2 * i, y[:, RANK:])
    for z in range(8):
        add(12 + z, mm_nt(get(4 + z).astype(BF16), tt[8 + z * 2 + (x >> 1)]))
    for z in range(8):
        add(20 + z, mm_nt(get(12 + z).astype(BF16), tt[24 + z * 4 + x]))
    for z in range(8):
        pair = tt[pl.ds(56 + z * 8 + x * 2, 2)].reshape(2 * RANK, RANK)
        y = mm_nt(get(20 + z).astype(BF16), pair)
        add(28 + 2 * z, y[:, 0:RANK])
        add(29 + 2 * z, y[:, RANK:])
    root[...] = jnp.zeros_like(root)
    for q in range(GROUP):
        for r in range(ROWS):
            msg[q, :, r * RANK : (r + 1) * RANK] = acc[
                r * total + q * 16 : r * total + (q + 1) * 16, :
            ].astype(BF16)
        root[q * 16 : q * 16 + ROWS, :] = get(28 + q)
        msg[q, :, LANES:] = root[q * 16 : (q + 1) * 16, :].astype(BF16)


def spread_kernel(msg, basis, trans, out, panels, root):
    for j in range(GROUP):
        for r in range(ROWS):
            panels[r * 256 + j * 16 : r * 256 + (j + 1) * 16, :] = msg[
                j, :, r * RANK : (r + 1) * RANK
            ].astype(F32)
        root[pl.ds(j, ROWS, stride=GROUP), :] = msg[j, :, LANES:].astype(F32)[0:ROWS]
    current = [root[...]]
    count = 2
    while count <= LD:
        below = []
        for h in range(count // 2):
            at = count - 2 + 2 * h
            y = mm_nt(current[h].astype(BF16), trans[at : at + 2].reshape(2 * RANK, RANK))
            below += [y[:, 0:RANK], y[:, RANK:]]
        current = below
        count *= 2
    for g in range(LD):
        coupled = jnp.concatenate(
            [panels[pl.ds(r * 256 + g, GROUP, stride=16), :] for r in range(ROWS)], axis=0
        )
        w = (current[g] + coupled).astype(BF16)
        out[:, g * RANK : (g + 1) * RANK] = mm_nt(w, basis[g * RANK : (g + 1) * RANK, :]).astype(
            BF16
        )


SMEM = pl.BlockSpec(memory_space=pltpu.SMEM)
WHOLE = pl.BlockSpec(memory_space=pltpu.VMEM)


def params(mib):
    return pltpu.CompilerParams(vmem_limit_bytes=mib * 1024 * 1024)


def cost(flops, moved):
    return pl.CostEstimate(flops=flops, bytes_accessed=moved, transcendentals=0)


def shards(
    rhs_block,
    leaf_basis,
    local_transfer,
    top_transfer,
    coupling_tiles,
    send_index,
    leaf_list,
    top_list,
):
    x = lax.axis_index("x")
    xme = x.astype(jnp.int32).reshape(1)
    trans = local_transfer.reshape(30, RANK, RANK)
    yme = lax.axis_index("rhs").astype(jnp.int32).reshape(1)
    near = lax.ppermute(coupling_tiles, "rhs", [(i, i ^ 1) for i in range(4)])
    over = lax.ppermute(coupling_tiles, "rhs", [(i, i ^ 3) for i in range(4)])
    msg = pl.pallas_call(
        gather_kernel,
        out_shape=jax.ShapeDtypeStruct((GROUP, LD, 1024), BF16),
        in_specs=[SMEM] + [WHOLE] * 4,
        out_specs=WHOLE,
        scratch_shapes=[pltpu.VMEM((1024, RANK), F32), pltpu.VMEM((256, RANK), F32)],
        compiler_params=params(60),
        name="leaf_panels",
    )(xme, rhs_block, leaf_basis, trans, leaf_list)
    msg = lax.all_to_all(msg, ("z", "core"), 0, 0, tiled=True)
    mine = pl.pallas_call(
        pack_kernel,
        out_shape=jax.ShapeDtypeStruct((272, LANES), BF16),
        in_specs=[WHOLE],
        out_specs=WHOLE,
        scratch_shapes=[pltpu.VMEM((256, RANK), F32)],
        compiler_params=params(4),
        name="pack",
    )(msg)
    blocks = [mine] + [
        lax.ppermute(mine, "x", [(i, (i + s) % 4) for i in range(4)]) for s in (1, 2, 3)
    ]
    sel, top_counts = pl.pallas_call(
        choice_kernel,
        out_shape=(
            jax.ShapeDtypeStruct((4, 1024, 256), BF16),
            jax.ShapeDtypeStruct((TILES * TARGETS, 128), BF16),
        ),
        in_specs=[SMEM] + [WHOLE] * 2,
        out_specs=(WHOLE, WHOLE),
        scratch_shapes=[pltpu.VMEM((256, 64), F32)],
        compiler_params=params(56),
        cost_estimate=cost(400_000_000, 3_000_000),
        name="choices",
    )(xme, send_index.transpose(0, 2, 1), top_list)
    near, top_counts = lax.optimization_barrier((near, top_counts))
    across = lax.ppermute(near, "rhs", [(i, i ^ 3) for i in range(4)])
    tables = (coupling_tiles, near, across, over)
    counts = pl.pallas_call(
        tally_kernel,
        out_shape=jax.ShapeDtypeStruct((GROUP, 1024, 256), BF16),
        in_specs=[WHOLE],
        out_specs=WHOLE,
        scratch_shapes=[pltpu.VMEM((1024, 128), F32)] * 4,
        compiler_params=params(6),
        cost_estimate=cost(4_000_000_000, 12_000_000),
        name="tallies",
    )(msg)
    total = 256 + TARGETS
    back = pl.pallas_call(
        couple_kernel,
        out_shape=jax.ShapeDtypeStruct((GROUP, LD, 640), BF16),
        in_specs=[SMEM] * 2 + [WHOLE] * 12,
        out_specs=WHOLE,
        scratch_shapes=[
            pltpu.VMEM((GROUP, 256, LANES), BF16),
            pltpu.VMEM((TILES, 19, 16, LANES), BF16),
            pltpu.VMEM((ROWS * 128, RANK), F32),
            pltpu.VMEM((ROWS * total, RANK), F32),
            pltpu.VMEM((GROUP * 16, RANK), F32),
        ],
        compiler_params=params(28),
        cost_estimate=cost(8_000_000_000, 20_000_000),
        name="interactions",
    )(xme, yme, *blocks, sel, counts, top_counts, *tables, top_transfer)
    back = lax.all_to_all(back, ("z", "core"), 0, 0, tiled=True)
    return pl.pallas_call(
        spread_kernel,
        out_shape=jax.ShapeDtypeStruct(rhs_block.shape, BF16),
        in_specs=[WHOLE] * 3,
        out_specs=WHOLE,
        scratch_shapes=[pltpu.VMEM((1024, RANK), F32), pltpu.VMEM((64, RANK), F32)],
        compiler_params=params(8),
        name="far_field",
    )(back, leaf_basis, trans)


def solution(mesh):
    grid = Mesh(mesh.devices.reshape(8, 4, 2, 4), ("z", "x", "core", "rhs"))
    leaf = ("z", "x", "core")
    placed = (
        P("rhs", leaf),
        P(leaf, None),
        P(leaf, None, None, None),
        P(),
        P("rhs", None, None),
        P(),
        P(None, leaf, None),
        P(),
    )
    return jax.shard_map(
        shards, mesh=grid, in_specs=placed, out_specs=P("rhs", leaf), check_vma=False
    )
```

```python
import functools

import jax
import jax.numpy as jnp
from jax import lax
from jax.experimental import pallas as pl
from jax.experimental.pallas import tpu as pltpu
from jax.sharding import Mesh, PartitionSpec as P

F32 = jnp.float32
BF16 = jnp.bfloat16
RANK = 128
LD = 16
TILES = 64
ENT = 192
GROUP = 16
ROWS = 4
TARGETS = 48
LANES = ROWS * RANK
CHUNK = 32
DEPTH = 16


def mm(a, b):
    return jnp.dot(a, b, preferred_element_type=F32)


def mm_nt(a, b):
    return lax.dot_general(a, b, (((1,), (1,)), ((), ())), preferred_element_type=F32)


def gather_kernel(xme, rhs, basis, trans, lists, msg, panels, root):
    x = xme[0]
    current = []
    for g in range(LD):
        panel = mm(rhs[:, g * RANK : (g + 1) * RANK], basis[g * RANK : (g + 1) * RANK, :])
        panels[g * 64 : (g + 1) * 64, :] = panel
        current.append(panel.astype(BF16))
    count = LD
    while count > 1:
        above = []
        for h in range(count // 2):
            pair = jnp.concatenate([current[2 * h], current[2 * h + 1]], axis=1)
            at = count - 2 + 2 * h
            above.append(mm(pair, trans[at : at + 2].reshape(2 * RANK, RANK)))
        current = [a.astype(BF16) for a in above]
        count //= 2
    root[...] = jnp.zeros_like(root)
    root[0:64, :] = above[0]
    slot = lists[0]
    p = slot >> 2
    slot = ((x - (p >> 1)) & 3) * 64 + (p >> 3) * 8 + (p & 1) * 4 + (slot & 3)
    slot = slot.astype(F32)
    tile = lists[1].astype(F32)
    codes = jnp.concatenate([slot, tile], axis=1).astype(BF16)
    for j in range(GROUP):
        msg[j, :, 0 : 2 * ENT] = codes
        msg[j, :, 384:512] = root[pl.ds(j, 16, stride=16), :].astype(BF16)
        for r in range(ROWS):
            msg[j, :, 512 + r * RANK : 512 + (r + 1) * RANK] = panels[
                pl.ds(r * GROUP + j, LD, stride=64), :
            ].astype(BF16)


def pack_kernel(msg, out, root):
    out[0:256, :] = msg[:, :, 512:1024].reshape(256, LANES)
    root[...] = msg[:, :, 384:512].reshape(256, RANK).astype(F32)
    for r in range(ROWS):
        out[256:272, r * RANK : (r + 1) * RANK] = root[pl.ds(r, GROUP, stride=LD), :].astype(BF16)


def choice_kernel(xme, index, top, sel, top_counts, rows):
    x = xme[0]
    for s in range(4):
        for q in range(GROUP):
            p = (q >> 1) * 8 + ((x - s) & 3) * 2 + (q & 1)
            rows[s * 64 + q * 4 : s * 64 + q * 4 + 4, :] = index[p].astype(F32)
    d = lax.broadcasted_iota(jnp.int32, (64, GROUP), 0)
    t = lax.broadcasted_iota(jnp.int32, (64, GROUP), 1)
    mine = jnp.where(d == (t >> 1) * 8 + x * 2 + (t & 1), 1.0, 0.0).astype(BF16)
    picks = mm(rows[...].astype(BF16), mine)
    place = lax.broadcasted_iota(jnp.int32, (256, GROUP), 0)
    picks = jnp.where(picks >= 0, picks + ((place >> 2) & 15).astype(F32) * 16, -1.0)
    lane = lax.broadcasted_iota(jnp.int32, (256, 256), 1).astype(F32)
    for t in range(GROUP):
        hot = jnp.where(picks[:, t : t + 1] == lane, 1.0, 0.0).astype(BF16)
        for s in range(4):
            sel[s, t * 64 : (t + 1) * 64, :] = hot[s * 64 : (s + 1) * 64, :]
    n = top[0:1, :]
    source = top[1:2, :]
    tile = top[2:3, :]
    m16 = n - 16
    m32 = n - 32
    m64 = n - 64
    at = jnp.where(
        n >= 16, jnp.where((m16 & 1) == (x >> 1), 12 + (m16 >> 1), -1), n - 4
    )
    at = jnp.where(n >= 32, jnp.where((m32 & 3) == x, 20 + (m32 >> 2), -1), at)
    at = jnp.where(
        n >= 64,
        jnp.where(((m64 >> 1) & 3) == x, 28 + (m64 >> 3) * 2 + (m64 & 1), -1),
        at,
    )
    code = jnp.where(at >= 0, tile * TARGETS + at, -1)
    width = top.shape[1]
    node = lax.broadcasted_iota(jnp.int32, (128, width), 0)
    source_hot = jnp.where(source == node, 1.0, 0.0).astype(BF16)
    part = 8 * TARGETS
    rows = lax.broadcasted_iota(jnp.int32, (part, width), 0)
    for b in range(8):
        hot = jnp.where(code == rows + b * part, 1.0, 0.0).astype(BF16)
        top_counts[b * part : (b + 1) * part, :] = mm_nt(hot, source_hot).astype(BF16)


def tally_kernel(lists, counts, low0, high0, low1, high1):
    one = jnp.ones((), BF16)
    zero = jnp.zeros((), BF16)
    low_ids = lax.broadcasted_iota(jnp.int32, (ENT, 128), 1).astype(F32).astype(BF16)
    high_ids = low_ids + 128
    tile_ids = lax.broadcasted_iota(jnp.int32, (TILES, ENT), 0).astype(F32).astype(BF16)

    def settle(low, high, d, g):
        rows = slice(g * TILES, (g + 1) * TILES)
        counts[d, rows, 0:128] = low[rows, :].astype(BF16)
        counts[d, rows, 128:256] = high[rows, :].astype(BF16)

    def device(d, low, high, low_before, high_before):
        codes = lists[d].astype(F32)
        slots = jnp.transpose(codes[:, 0:256])
        tiles = codes[:, ENT : 2 * ENT]
        for g in range(LD):
            slot = jnp.broadcast_to(slots[0:ENT, g : g + 1], (ENT, 128)).astype(BF16)
            slot_hot = jnp.concatenate(
                [jnp.where(slot == low_ids, one, zero), jnp.where(slot == high_ids, one, zero)],
                axis=1,
            )
            tile = tiles[g : g + 1, :].astype(BF16)
            tally = mm(jnp.where(tile == tile_ids, one, zero), slot_hot)
            low[pl.ds(g, TILES, stride=LD), :] = tally[:, 0:128]
            high[pl.ds(g, TILES, stride=LD), :] = tally[:, 128:256]
            settle(low_before, high_before, jnp.maximum(d - 1, 0), g)

    low1[...] = jnp.zeros_like(low1)
    high1[...] = jnp.zeros_like(high1)

    def two(i, carry):
        device(2 * i, low0, high0, low1, high1)
        device(2 * i + 1, low1, high1, low0, high0)
        return carry

    lax.fori_loop(0, GROUP // 2, two, 0)
    for g in range(LD):
        settle(low1, high1, GROUP - 1, g)


def couple_kernel(
    xme,
    yme,
    a0,
    a1,
    a2,
    a3,
    sel,
    counts,
    top_counts,
    t0,
    t1,
    t2,
    t3,
    tt,
    msg,
    pool,
    zs,
    xtop,
    acc,
    root,
):
    x = xme[0]
    total = 256 + TARGETS
    held = (a0, a1, a2, a3)
    xtop[...] = jnp.zeros_like(xtop)
    acc[...] = jnp.zeros_like(acc)
    for s in range(4):
        panels = held[s][0:256, :]
        got = mm(sel[s], panels).astype(BF16)
        for t in range(GROUP):
            pool[t, s * 64 : (s + 1) * 64, :] = got[t * 64 : (t + 1) * 64, :]

    def device(d, carry):
        for m in range(TILES // CHUNK):
            z = mm(counts[d, m * CHUNK * 16 : (m + 1) * CHUNK * 16, :], pool[d]).astype(BF16)
            zs[m * CHUNK : (m + 1) * CHUNK, d] = z.reshape(CHUNK, 16, LANES)
        return carry

    lax.fori_loop(0, GROUP, device, 0, unroll=4)
    for s in range(4):
        for r in range(ROWS):
            root[0:GROUP, :] = held[s][256:272, r * RANK : (r + 1) * RANK].astype(F32)
            for z in range(8):
                n = 64 + z * 8 + ((x - s) & 3) * 2
                xtop[pl.ds(r * 128 + n, 2), :] = root[2 * z : 2 * z + 2, :]
    for n in range(63, 3, -1):
        left = xtop[pl.ds(2 * n, ROWS, stride=128), :]
        right = xtop[pl.ds(2 * n + 1, ROWS, stride=128), :]
        pair = jnp.concatenate([left, right], axis=1).astype(BF16)
        up = mm(pair, tt[2 * n - 8 : 2 * n - 6].reshape(2 * RANK, RANK))
        xtop[pl.ds(n, ROWS, stride=128), :] = up.astype(BF16).astype(F32)
    sources = jnp.concatenate(
        [xtop[r * 128 : (r + 1) * 128, :] for r in range(ROWS)], axis=1
    ).astype(BF16)
    part = 8 * TARGETS
    for b in range(8):
        z = mm(top_counts[b * part : (b + 1) * part, :], sources).astype(BF16)
        zs[b * 8 : (b + 1) * 8, 16:19] = z.reshape(8, 3, 16, LANES)

    for y, table in enumerate((t0, t1, t2, t3)):
        first = (yme[0] ^ y) * 16

        def step(i, carry):
            k = i * DEPTH
            tiles = table[pl.ds(k, DEPTH)].reshape(DEPTH * RANK, RANK)
            for r in range(ROWS):
                lanes = slice(r * RANK, (r + 1) * RANK)
                wide = jnp.concatenate(
                    [zs[first + k + h, :, :, lanes].reshape(total, RANK) for h in range(DEPTH)],
                    axis=1,
                )
                acc[r * total : (r + 1) * total, :] += mm(wide, tiles)
            return carry

        lax.fori_loop(0, 16 // DEPTH, step, 0)

    def get(t):
        return acc[pl.ds(256 + t, ROWS, stride=total), :]

    def add(t, value):
        acc[pl.ds(256 + t, ROWS, stride=total), :] += value

    for i in range(4):
        y = mm_nt(get(i).astype(BF16), tt[2 * i : 2 * i + 2].reshape(2 * RANK, RANK))
        add(4 + 2 * i, y[:, 0:RANK])
        add(5 + 2 * i, y[:, RANK:])
    for z in range(8):
        add(12 + z, mm_nt(get(4 + z).astype(BF16), tt[8 + z * 2 + (x >> 1)]))
    for z in range(8):
        add(20 + z, mm_nt(get(12 + z).astype(BF16), tt[24 + z * 4 + x]))
    for z in range(8):
        pair = tt[pl.ds(56 + z * 8 + x * 2, 2)].reshape(2 * RANK, RANK)
        y = mm_nt(get(20 + z).astype(BF16), pair)
        add(28 + 2 * z, y[:, 0:RANK])
        add(29 + 2 * z, y[:, RANK:])
    root[...] = jnp.zeros_like(root)
    for q in range(GROUP):
        for r in range(ROWS):
            msg[q, :, r * RANK : (r + 1) * RANK] = acc[
                r * total + q * 16 : r * total + (q + 1) * 16, :
            ].astype(BF16)
        root[q * 16 : q * 16 + ROWS, :] = get(28 + q)
        msg[q, :, LANES:] = root[q * 16 : (q + 1) * 16, :].astype(BF16)


def spread_kernel(msg, basis, trans, out, panels, root):
    for j in range(GROUP):
        for r in range(ROWS):
            panels[r * 256 + j * 16 : r * 256 + (j + 1) * 16, :] = msg[
                j, :, r * RANK : (r + 1) * RANK
            ].astype(F32)
        root[pl.ds(j, ROWS, stride=GROUP), :] = msg[j, :, LANES:].astype(F32)[0:ROWS]
    current = [root[...]]
    count = 2
    while count <= LD:
        below = []
        for h in range(count // 2):
            at = count - 2 + 2 * h
            y = mm_nt(current[h].astype(BF16), trans[at : at + 2].reshape(2 * RANK, RANK))
            below += [y[:, 0:RANK], y[:, RANK:]]
        current = below
        count *= 2
    for g in range(LD):
        coupled = jnp.concatenate(
            [panels[pl.ds(r * 256 + g, GROUP, stride=16), :] for r in range(ROWS)], axis=0
        )
        w = (current[g] + coupled).astype(BF16)
        out[:, g * RANK : (g + 1) * RANK] = mm_nt(w, basis[g * RANK : (g + 1) * RANK, :]).astype(
            BF16
        )


SMEM = pl.BlockSpec(memory_space=pltpu.SMEM)
WHOLE = pl.BlockSpec(memory_space=pltpu.VMEM)


def params(mib):
    return pltpu.CompilerParams(vmem_limit_bytes=mib * 1024 * 1024)


def cost(flops, moved):
    return pl.CostEstimate(flops=flops, bytes_accessed=moved, transcendentals=0)


def shards(
    rhs_block,
    leaf_basis,
    local_transfer,
    top_transfer,
    coupling_tiles,
    send_index,
    leaf_list,
    top_list,
):
    x = lax.axis_index("x")
    xme = x.astype(jnp.int32).reshape(1)
    trans = local_transfer.reshape(30, RANK, RANK)
    yme = lax.axis_index("rhs").astype(jnp.int32).reshape(1)
    near = lax.ppermute(coupling_tiles, "rhs", [(i, i ^ 1) for i in range(4)])
    over = lax.ppermute(coupling_tiles, "rhs", [(i, i ^ 3) for i in range(4)])
    msg = pl.pallas_call(
        gather_kernel,
        out_shape=jax.ShapeDtypeStruct((GROUP, LD, 1024), BF16),
        in_specs=[SMEM] + [WHOLE] * 4,
        out_specs=WHOLE,
        scratch_shapes=[pltpu.VMEM((1024, RANK), F32), pltpu.VMEM((256, RANK), F32)],
        compiler_params=params(60),
        name="leaf_panels",
    )(xme, rhs_block, leaf_basis, trans, leaf_list)
    msg = lax.all_to_all(msg, ("z", "core"), 0, 0, tiled=True)
    mine = pl.pallas_call(
        pack_kernel,
        out_shape=jax.ShapeDtypeStruct((272, LANES), BF16),
        in_specs=[WHOLE],
        out_specs=WHOLE,
        scratch_shapes=[pltpu.VMEM((256, RANK), F32)],
        compiler_params=params(4),
        name="pack",
    )(msg)
    blocks = [mine] + [
        lax.ppermute(mine, "x", [(i, (i + s) % 4) for i in range(4)]) for s in (1, 2, 3)
    ]
    sel, top_counts = pl.pallas_call(
        choice_kernel,
        out_shape=(
            jax.ShapeDtypeStruct((4, 1024, 256), BF16),
            jax.ShapeDtypeStruct((TILES * TARGETS, 128), BF16),
        ),
        in_specs=[SMEM] + [WHOLE] * 2,
        out_specs=(WHOLE, WHOLE),
        scratch_shapes=[pltpu.VMEM((256, 64), F32)],
        compiler_params=params(56),
        cost_estimate=cost(400_000_000, 3_000_000),
        name="choices",
    )(xme, send_index.transpose(0, 2, 1), top_list)
    near, top_counts = lax.optimization_barrier((near, top_counts))
    across = lax.ppermute(near, "rhs", [(i, i ^ 3) for i in range(4)])
    tables = (coupling_tiles, near, across, over)
    counts = pl.pallas_call(
        tally_kernel,
        out_shape=jax.ShapeDtypeStruct((GROUP, 1024, 256), BF16),
        in_specs=[WHOLE],
        out_specs=WHOLE,
        scratch_shapes=[pltpu.VMEM((1024, 128), F32)] * 4,
        compiler_params=params(6),
        cost_estimate=cost(4_000_000_000, 12_000_000),
        name="tallies",
    )(msg)
    total = 256 + TARGETS
    back = pl.pallas_call(
        couple_kernel,
        out_shape=jax.ShapeDtypeStruct((GROUP, LD, 640), BF16),
        in_specs=[SMEM] * 2 + [WHOLE] * 12,
        out_specs=WHOLE,
        scratch_shapes=[
            pltpu.VMEM((GROUP, 256, LANES), BF16),
            pltpu.VMEM((TILES, 19, 16, LANES), BF16),
            pltpu.VMEM((ROWS * 128, RANK), F32),
            pltpu.VMEM((ROWS * total, RANK), F32),
            pltpu.VMEM((GROUP * 16, RANK), F32),
        ],
        compiler_params=params(28),
        cost_estimate=cost(8_000_000_000, 20_000_000),
        name="interactions",
    )(xme, yme, *blocks, sel, counts, top_counts, *tables, top_transfer)
    back = lax.all_to_all(back, ("z", "core"), 0, 0, tiled=True)
    return pl.pallas_call(
        spread_kernel,
        out_shape=jax.ShapeDtypeStruct(rhs_block.shape, BF16),
        in_specs=[WHOLE] * 3,
        out_specs=WHOLE,
        scratch_shapes=[pltpu.VMEM((1024, RANK), F32), pltpu.VMEM((64, RANK), F32)],
        compiler_params=params(8),
        name="far_field",
    )(back, leaf_basis, trans)


def solution(mesh):
    grid = Mesh(mesh.devices.reshape(8, 4, 2, 4), ("z", "x", "core", "rhs"))
    leaf = ("z", "x", "core")
    placed = (
        P("rhs", leaf),
        P(leaf, None),
        P(leaf, None, None, None),
        P(),
        P("rhs", None, None),
        P(),
        P(None, leaf, None),
        P(),
    )
    return jax.shard_map(
        shards, mesh=grid, in_specs=placed, out_specs=P("rhs", leaf), check_vma=False
    )
```

```python
import functools

import jax
import jax.numpy as jnp
from jax import lax
from jax.experimental import pallas as pl
from jax.experimental.pallas import tpu as pltpu
from jax.sharding import Mesh, PartitionSpec as P

F32 = jnp.float32
BF16 = jnp.bfloat16
RANK = 128
LD = 16
TILES = 64
ENT = 192
GROUP = 16
ROWS = 4
TARGETS = 48
LANES = ROWS * RANK
CHUNK = 32
DEPTH = 16


def mm(a, b):
    return jnp.dot(a, b, preferred_element_type=F32)


def mm_nt(a, b):
    return lax.dot_general(a, b, (((1,), (1,)), ((), ())), preferred_element_type=F32)


def gather_kernel(xme, rhs, basis, trans, lists, msg, panels, root):
    x = xme[0]
    current = []
    for g in range(LD):
        panel = mm(rhs[:, g * RANK : (g + 1) * RANK], basis[g * RANK : (g + 1) * RANK, :])
        panels[g * 64 : (g + 1) * 64, :] = panel
        current.append(panel.astype(BF16))
    count = LD
    while count > 1:
        above = []
        for h in range(count // 2):
            pair = jnp.concatenate([current[2 * h], current[2 * h + 1]], axis=1)
            at = count - 2 + 2 * h
            above.append(mm(pair, trans[at : at + 2].reshape(2 * RANK, RANK)))
        current = [a.astype(BF16) for a in above]
        count //= 2
    root[...] = jnp.zeros_like(root)
    root[0:64, :] = above[0]
    slot = lists[0]
    p = slot >> 2
    slot = ((x - (p >> 1)) & 3) * 64 + (p >> 3) * 8 + (p & 1) * 4 + (slot & 3)
    slot = slot.astype(F32)
    tile = lists[1].astype(F32)
    codes = jnp.concatenate([slot, tile], axis=1).astype(BF16)
    for j in range(GROUP):
        msg[j, :, 0 : 2 * ENT] = codes
        msg[j, :, 384:512] = root[pl.ds(j, 16, stride=16), :].astype(BF16)
        for r in range(ROWS):
            msg[j, :, 512 + r * RANK : 512 + (r + 1) * RANK] = panels[
                pl.ds(r * GROUP + j, LD, stride=64), :
            ].astype(BF16)


def pack_kernel(msg, out, root):
    out[0:256, :] = msg[:, :, 512:1024].reshape(256, LANES)
    root[...] = msg[:, :, 384:512].reshape(256, RANK).astype(F32)
    for r in range(ROWS):
        out[256:272, r * RANK : (r + 1) * RANK] = root[pl.ds(r, GROUP, stride=LD), :].astype(BF16)


def choice_kernel(xme, index, top, sel, top_counts, rows):
    x = xme[0]
    for s in range(4):
        for q in range(GROUP):
            p = (q >> 1) * 8 + ((x - s) & 3) * 2 + (q & 1)
            rows[s * 64 + q * 4 : s * 64 + q * 4 + 4, :] = index[p].astype(F32)
    d = lax.broadcasted_iota(jnp.int32, (64, GROUP), 0)
    t = lax.broadcasted_iota(jnp.int32, (64, GROUP), 1)
    mine = jnp.where(d == (t >> 1) * 8 + x * 2 + (t & 1), 1.0, 0.0).astype(BF16)
    picks = mm(rows[...].astype(BF16), mine)
    place = lax.broadcasted_iota(jnp.int32, (256, GROUP), 0)
    picks = jnp.where(picks >= 0, picks + ((place >> 2) & 15).astype(F32) * 16, -1.0)
    lane = lax.broadcasted_iota(jnp.int32, (256, 256), 1).astype(F32)
    for t in range(GROUP):
        hot = jnp.where(picks[:, t : t + 1] == lane, 1.0, 0.0).astype(BF16)
        for s in range(4):
            sel[s, t * 64 : (t + 1) * 64, :] = hot[s * 64 : (s + 1) * 64, :]
    n = top[0:1, :]
    source = top[1:2, :]
    tile = top[2:3, :]
    m16 = n - 16
    m32 = n - 32
    m64 = n - 64
    at = jnp.where(
        n >= 16, jnp.where((m16 & 1) == (x >> 1), 12 + (m16 >> 1), -1), n - 4
    )
    at = jnp.where(n >= 32, jnp.where((m32 & 3) == x, 20 + (m32 >> 2), -1), at)
    at = jnp.where(
        n >= 64,
        jnp.where(((m64 >> 1) & 3) == x, 28 + (m64 >> 3) * 2 + (m64 & 1), -1),
        at,
    )
    code = jnp.where(at >= 0, tile * TARGETS + at, -1)
    width = top.shape[1]
    node = lax.broadcasted_iota(jnp.int32, (128, width), 0)
    source_hot = jnp.where(source == node, 1.0, 0.0).astype(BF16)
    part = 8 * TARGETS
    rows = lax.broadcasted_iota(jnp.int32, (part, width), 0)
    for b in range(8):
        hot = jnp.where(code == rows + b * part, 1.0, 0.0).astype(BF16)
        top_counts[b * part : (b + 1) * part, :] = mm_nt(hot, source_hot).astype(BF16)


def tally_kernel(lists, counts, low0, high0, low1, high1):
    one = jnp.ones((), BF16)
    zero = jnp.zeros((), BF16)
    low_ids = lax.broadcasted_iota(jnp.int32, (ENT, 128), 1).astype(F32).astype(BF16)
    high_ids = low_ids + 128
    tile_ids = lax.broadcasted_iota(jnp.int32, (TILES, ENT), 0).astype(F32).astype(BF16)

    def settle(low, high, d, g):
        rows = slice(g * TILES, (g + 1) * TILES)
        counts[d, rows, 0:128] = low[rows, :].astype(BF16)
        counts[d, rows, 128:256] = high[rows, :].astype(BF16)

    def device(d, low, high, low_before, high_before):
        codes = lists[d].astype(F32)
        slots = jnp.transpose(codes[:, 0:256])
        tiles = codes[:, ENT : 2 * ENT]
        for g in range(LD):
            slot = jnp.broadcast_to(slots[0:ENT, g : g + 1], (ENT, 128)).astype(BF16)
            slot_hot = jnp.concatenate(
                [jnp.where(slot == low_ids, one, zero), jnp.where(slot == high_ids, one, zero)],
                axis=1,
            )
            tile = tiles[g : g + 1, :].astype(BF16)
            tally = mm(jnp.where(tile == tile_ids, one, zero), slot_hot)
            low[pl.ds(g, TILES, stride=LD), :] = tally[:, 0:128]
            high[pl.ds(g, TILES, stride=LD), :] = tally[:, 128:256]
            settle(low_before, high_before, jnp.maximum(d - 1, 0), g)

    low1[...] = jnp.zeros_like(low1)
    high1[...] = jnp.zeros_like(high1)

    def two(i, carry):
        device(2 * i, low0, high0, low1, high1)
        device(2 * i + 1, low1, high1, low0, high0)
        return carry

    lax.fori_loop(0, GROUP // 2, two, 0, unroll=2)
    for g in range(LD):
        settle(low1, high1, GROUP - 1, g)


def couple_kernel(
    xme,
    yme,
    a0,
    a1,
    a2,
    a3,
    sel,
    counts,
    top_counts,
    t0,
    t1,
    t2,
    t3,
    tt,
    msg,
    pool,
    zs,
    xtop,
    acc,
    root,
):
    x = xme[0]
    total = 256 + TARGETS
    held = (a0, a1, a2, a3)
    xtop[...] = jnp.zeros_like(xtop)
    acc[...] = jnp.zeros_like(acc)
    for s in range(4):
        panels = held[s][0:256, :]
        got = mm(sel[s], panels).astype(BF16)
        for t in range(GROUP):
            pool[t, s * 64 : (s + 1) * 64, :] = got[t * 64 : (t + 1) * 64, :]

    def device(d, carry):
        for m in range(TILES // CHUNK):
            z = mm(counts[d, m * CHUNK * 16 : (m + 1) * CHUNK * 16, :], pool[d]).astype(BF16)
            zs[m * CHUNK : (m + 1) * CHUNK, d] = z.reshape(CHUNK, 16, LANES)
        return carry

    lax.fori_loop(0, GROUP, device, 0, unroll=4)
    for s in range(4):
        for r in range(ROWS):
            root[0:GROUP, :] = held[s][256:272, r * RANK : (r + 1) * RANK].astype(F32)
            for z in range(8):
                n = 64 + z * 8 + ((x - s) & 3) * 2
                xtop[pl.ds(r * 128 + n, 2), :] = root[2 * z : 2 * z + 2, :]
    for n in range(63, 3, -1):
        left = xtop[pl.ds(2 * n, ROWS, stride=128), :]
        right = xtop[pl.ds(2 * n + 1, ROWS, stride=128), :]
        pair = jnp.concatenate([left, right], axis=1).astype(BF16)
        up = mm(pair, tt[2 * n - 8 : 2 * n - 6].reshape(2 * RANK, RANK))
        xtop[pl.ds(n, ROWS, stride=128), :] = up.astype(BF16).astype(F32)
    sources = jnp.concatenate(
        [xtop[r * 128 : (r + 1) * 128, :] for r in range(ROWS)], axis=1
    ).astype(BF16)
    part = 8 * TARGETS
    for b in range(8):
        z = mm(top_counts[b * part : (b + 1) * part, :], sources).astype(BF16)
        zs[b * 8 : (b + 1) * 8, 16:19] = z.reshape(8, 3, 16, LANES)

    for y, table in enumerate((t0, t1, t2, t3)):
        first = (yme[0] ^ y) * 16

        def step(i, carry):
            k = i * DEPTH
            tiles = table[pl.ds(k, DEPTH)].reshape(DEPTH * RANK, RANK)
            for r in range(ROWS):
                lanes = slice(r * RANK, (r + 1) * RANK)
                wide = jnp.concatenate(
                    [zs[first + k + h, :, :, lanes].reshape(total, RANK) for h in range(DEPTH)],
                    axis=1,
                )
                acc[r * total : (r + 1) * total, :] += mm(wide, tiles)
            return carry

        lax.fori_loop(0, 16 // DEPTH, step, 0)

    def get(t):
        return acc[pl.ds(256 + t, ROWS, stride=total), :]

    def add(t, value):
        acc[pl.ds(256 + t, ROWS, stride=total), :] += value

    for i in range(4):
        y = mm_nt(get(i).astype(BF16), tt[2 * i : 2 * i + 2].reshape(2 * RANK, RANK))
        add(4 + 2 * i, y[:, 0:RANK])
        add(5 + 2 * i, y[:, RANK:])
    for z in range(8):
        add(12 + z, mm_nt(get(4 + z).astype(BF16), tt[8 + z * 2 + (x >> 1)]))
    for z in range(8):
        add(20 + z, mm_nt(get(12 + z).astype(BF16), tt[24 + z * 4 + x]))
    for z in range(8):
        pair = tt[pl.ds(56 + z * 8 + x * 2, 2)].reshape(2 * RANK, RANK)
        y = mm_nt(get(20 + z).astype(BF16), pair)
        add(28 + 2 * z, y[:, 0:RANK])
        add(29 + 2 * z, y[:, RANK:])
    root[...] = jnp.zeros_like(root)
    for q in range(GROUP):
        for r in range(ROWS):
            msg[q, :, r * RANK : (r + 1) * RANK] = acc[
                r * total + q * 16 : r * total + (q + 1) * 16, :
            ].astype(BF16)
        root[q * 16 : q * 16 + ROWS, :] = get(28 + q)
        msg[q, :, LANES:] = root[q * 16 : (q + 1) * 16, :].astype(BF16)


def spread_kernel(msg, basis, trans, out, panels, root):
    for j in range(GROUP):
        for r in range(ROWS):
            panels[r * 256 + j * 16 : r * 256 + (j + 1) * 16, :] = msg[
                j, :, r * RANK : (r + 1) * RANK
            ].astype(F32)
        root[pl.ds(j, ROWS, stride=GROUP), :] = msg[j, :, LANES:].astype(F32)[0:ROWS]
    current = [root[...]]
    count = 2
    while count <= LD:
        below = []
        for h in range(count // 2):
            at = count - 2 + 2 * h
            y = mm_nt(current[h].astype(BF16), trans[at : at + 2].reshape(2 * RANK, RANK))
            below += [y[:, 0:RANK], y[:, RANK:]]
        current = below
        count *= 2
    for g in range(LD):
        coupled = jnp.concatenate(
            [panels[pl.ds(r * 256 + g, GROUP, stride=16), :] for r in range(ROWS)], axis=0
        )
        w = (current[g] + coupled).astype(BF16)
        out[:, g * RANK : (g + 1) * RANK] = mm_nt(w, basis[g * RANK : (g + 1) * RANK, :]).astype(
            BF16
        )


SMEM = pl.BlockSpec(memory_space=pltpu.SMEM)
WHOLE = pl.BlockSpec(memory_space=pltpu.VMEM)


def params(mib):
    return pltpu.CompilerParams(vmem_limit_bytes=mib * 1024 * 1024)


def cost(flops, moved):
    return pl.CostEstimate(flops=flops, bytes_accessed=moved, transcendentals=0)


def shards(
    rhs_block,
    leaf_basis,
    local_transfer,
    top_transfer,
    coupling_tiles,
    send_index,
    leaf_list,
    top_list,
):
    x = lax.axis_index("x")
    xme = x.astype(jnp.int32).reshape(1)
    trans = local_transfer.reshape(30, RANK, RANK)
    yme = lax.axis_index("rhs").astype(jnp.int32).reshape(1)
    near = lax.ppermute(coupling_tiles, "rhs", [(i, i ^ 1) for i in range(4)])
    over = lax.ppermute(coupling_tiles, "rhs", [(i, i ^ 3) for i in range(4)])
    msg = pl.pallas_call(
        gather_kernel,
        out_shape=jax.ShapeDtypeStruct((GROUP, LD, 1024), BF16),
        in_specs=[SMEM] + [WHOLE] * 4,
        out_specs=WHOLE,
        scratch_shapes=[pltpu.VMEM((1024, RANK), F32), pltpu.VMEM((256, RANK), F32)],
        compiler_params=params(60),
        name="leaf_panels",
    )(xme, rhs_block, leaf_basis, trans, leaf_list)
    msg = lax.all_to_all(msg, ("z", "core"), 0, 0, tiled=True)
    mine = pl.pallas_call(
        pack_kernel,
        out_shape=jax.ShapeDtypeStruct((272, LANES), BF16),
        in_specs=[WHOLE],
        out_specs=WHOLE,
        scratch_shapes=[pltpu.VMEM((256, RANK), F32)],
        compiler_params=params(4),
        name="pack",
    )(msg)
    blocks = [mine] + [
        lax.ppermute(mine, "x", [(i, (i + s) % 4) for i in range(4)]) for s in (1, 2, 3)
    ]
    sel, top_counts = pl.pallas_call(
        choice_kernel,
        out_shape=(
            jax.ShapeDtypeStruct((4, 1024, 256), BF16),
            jax.ShapeDtypeStruct((TILES * TARGETS, 128), BF16),
        ),
        in_specs=[SMEM] + [WHOLE] * 2,
        out_specs=(WHOLE, WHOLE),
        scratch_shapes=[pltpu.VMEM((256, 64), F32)],
        compiler_params=params(56),
        cost_estimate=cost(400_000_000, 3_000_000),
        name="choices",
    )(xme, send_index.transpose(0, 2, 1), top_list)
    near, top_counts = lax.optimization_barrier((near, top_counts))
    across = lax.ppermute(near, "rhs", [(i, i ^ 3) for i in range(4)])
    tables = (coupling_tiles, near, across, over)
    counts = pl.pallas_call(
        tally_kernel,
        out_shape=jax.ShapeDtypeStruct((GROUP, 1024, 256), BF16),
        in_specs=[WHOLE],
        out_specs=WHOLE,
        scratch_shapes=[pltpu.VMEM((1024, 128), F32)] * 4,
        compiler_params=params(6),
        cost_estimate=cost(4_000_000_000, 12_000_000),
        name="tallies",
    )(msg)
    total = 256 + TARGETS
    back = pl.pallas_call(
        couple_kernel,
        out_shape=jax.ShapeDtypeStruct((GROUP, LD, 640), BF16),
        in_specs=[SMEM] * 2 + [WHOLE] * 12,
        out_specs=WHOLE,
        scratch_shapes=[
            pltpu.VMEM((GROUP, 256, LANES), BF16),
            pltpu.VMEM((TILES, 19, 16, LANES), BF16),
            pltpu.VMEM((ROWS * 128, RANK), F32),
            pltpu.VMEM((ROWS * total, RANK), F32),
            pltpu.VMEM((GROUP * 16, RANK), F32),
        ],
        compiler_params=params(28),
        cost_estimate=cost(8_000_000_000, 20_000_000),
        name="interactions",
    )(xme, yme, *blocks, sel, counts, top_counts, *tables, top_transfer)
    back = lax.all_to_all(back, ("z", "core"), 0, 0, tiled=True)
    return pl.pallas_call(
        spread_kernel,
        out_shape=jax.ShapeDtypeStruct(rhs_block.shape, BF16),
        in_specs=[WHOLE] * 3,
        out_specs=WHOLE,
        scratch_shapes=[pltpu.VMEM((1024, RANK), F32), pltpu.VMEM((64, RANK), F32)],
        compiler_params=params(8),
        name="far_field",
    )(back, leaf_basis, trans)


def solution(mesh):
    grid = Mesh(mesh.devices.reshape(8, 4, 2, 4), ("z", "x", "core", "rhs"))
    leaf = ("z", "x", "core")
    placed = (
        P("rhs", leaf),
        P(leaf, None),
        P(leaf, None, None, None),
        P(),
        P("rhs", None, None),
        P(),
        P(None, leaf, None),
        P(),
    )
    return jax.shard_map(
        shards, mesh=grid, in_specs=placed, out_specs=P("rhs", leaf), check_vma=False
    )
```
